32 devices in a mesh: groups: 2 (over y), freq: 4 (over z), read: 2 (over x), pair: 2 (over core).
Axes of the slice: x: 2, y: 2, z: 4, core: 2. Of those that a mesh axis runs over, the one named last changes fastest.
Arguments:
- exposures: float32 [8, 2048, 2048], P(('groups', 'read', 'pair'), 'freq'), parts along dimension 0, may hold values from -6 to 6
- stamps: float32 [8, 16, 16], P('groups'), parts along dimension 0, may hold values from -1 to 1, as said below
- zero_point: float32 [8], P('groups'), parts along dimension 0, may hold values from 0.5 to 2
- noise_var: float32 [8], P('groups'), parts along dimension 0, may hold values from 0.25 to 4
- footprint: int32 [8, 2], P('groups'), parts along dimension 0, may hold values from 0 to 2048, as said below
- accept: int32 [8], P('groups'), parts along dimension 0, may hold values from 0 to 1, as said below
- assign: int32 [8], P('groups'), parts along dimension 0, may hold values from 0 to 3, each once
Outputs:
- coadd: float32 [2, 4096, 1024], P(None, ('groups', 'read', 'pair'), 'freq'), parts along dimension 1
The draws below stay inside these ranges and needn't reach their ends.
There are 2 independent parts, one for each index of `groups`. The reference program is written for one: setup_inputs(seed, part) draws one part's arguments, and reference() takes and returns one part's arrays. A program takes and returns all parts, laid end to end along the dimension named above; each array names one. Nothing has to cross between parts.
Inputs may be any that keep to these rules, and one draw needn't show every extreme that they name: `stamps`: each stamp is 1 at row 8 and column 8, and the absolute values of its other entries sum to at most 0.9. For every exposure footprint[e, 0] < footprint[e, 1] and the two differ by at least 512; some exposure covers all 2048 rows. `accept`: at least one exposure is rejected, and at least one exposure that covers all 2048 rows is accepted. `assign`: each exposure sits in exactly one slot.
All inputs are finite; a program needn't handle non-finite values.
Results may differ from the reference program's by a relative error of at most 0.0001.
Values sent between devices are 32-bit elements; how exact they have to be, the bound alone decides.
A program may use at most 64 MiB of HBM per device.

```python
import math
import jax
import jax.numpy as jnp

HEIGHT = 2048
WIDTH = 2048
STAMP = 16
EXPOSURES = 4


def draw_stamps(key, part):
    sign_key = jax.random.fold_in(key, 11)
    size_key = jax.random.fold_in(key, 12)
    shape_all = (EXPOSURES, STAMP, STAMP)
    signs = jnp.where(jax.random.bernoulli(sign_key, 0.5, shape_all), 1.0, -1.0)
    magnitude = jax.random.uniform(size_key, shape_all, jnp.float32, 0.5, 1.0)
    wings = signs * magnitude * (0.9 / (STAMP * STAMP - 1))
    row_ids = jnp.arange(STAMP)
    centre = (row_ids[:, None] == STAMP // 2) & (row_ids[None, :] == STAMP // 2)
    return jnp.where(centre[None], 1.0, wings).astype(jnp.float32)


def full_exposure(key):
    return jax.random.randint(jax.random.fold_in(key, 23), (), 0, EXPOSURES)


def draw_footprint(key, part):
    span_key = jax.random.fold_in(key, 21)
    start_key = jax.random.fold_in(key, 22)
    full_one = full_exposure(key)
    span_rows = jax.random.randint(span_key, (EXPOSURES,), HEIGHT // 4, HEIGHT + 1)
    start_rows = jax.random.randint(start_key, (EXPOSURES,), 0, HEIGHT - span_rows + 1)
    picked = jnp.arange(EXPOSURES) == full_one
    span_rows = jnp.where(picked, HEIGHT, span_rows)
    start_rows = jnp.where(picked, 0, start_rows)
    return jnp.stack([start_rows, start_rows + span_rows], axis=1).astype(jnp.int32)


def draw_accept(key, part):
    flag_key = jax.random.fold_in(key, 31)
    step_key = jax.random.fold_in(key, 33)
    flags = (jax.random.randint(flag_key, (EXPOSURES,), 0, 4) > 0).astype(jnp.int32)
    forced_yes = full_exposure(key)
    forced_no = (forced_yes + 1 + jax.random.randint(step_key, (), 0, EXPOSURES - 1)) % EXPOSURES
    labels = jnp.arange(EXPOSURES)
    flags = jnp.where(labels == forced_yes, 1, flags)
    flags = jnp.where(labels == forced_no, 0, flags)
    return flags.astype(jnp.int32)


def shard_levels(stream_key, dims, split, smallest, top_value):
    factor_of = 1.0
    for axis_at, blocks in split:
        draws = jax.random.uniform(jax.random.fold_in(jax.random.fold_in(stream_key, 6), axis_at), (blocks,), jnp.float32, smallest / len(split), top_value / len(split))
        factor_of = factor_of * jnp.repeat(jnp.exp(draws), dims[axis_at] // blocks).reshape((-1,) + (1,) * (len(dims) - 1 - axis_at))
    return factor_of


def bell_draw(rng, shape, spread, reach, pieces=(), held_as=jnp.bfloat16):
    array = jax.random.normal(rng, shape, jnp.float32) * spread
    if len(pieces) > 0:
        array = shard_levels(rng, shape, pieces, -0.22, 0.18) * array
    return jnp.clip(array, min=-reach, max=reach).astype(held_as)


def setup_inputs(seed: int = 0, part: int = 0) -> dict:
    splits = jax.random.split(jax.random.key(seed), 8)
    part_splits = jax.random.split(jax.random.fold_in(splits[7], part), 8)
    return {
        "exposures": bell_draw(part_splits[0], (EXPOSURES, HEIGHT, WIDTH), 1.0, 6.0, ((0, 4), (1, 4)), jnp.float32),
        "stamps": draw_stamps(jax.random.fold_in(jax.random.fold_in(splits[7], part), 71), part),
        "zero_point": jnp.clip(jnp.exp(jax.random.uniform(part_splits[2], (EXPOSURES,), jnp.float32, math.log(0.5), math.log(2.0))), 0.5, 2.0),
        "noise_var": jnp.clip(jnp.exp(jax.random.uniform(part_splits[3], (EXPOSURES,), jnp.float32, math.log(0.25), math.log(4.0))), 0.25, 4.0),
        "footprint": draw_footprint(jax.random.fold_in(jax.random.fold_in(splits[7], part), 71), part),
        "accept": draw_accept(jax.random.fold_in(jax.random.fold_in(splits[7], part), 71), part),
        "assign": jax.random.permutation(part_splits[6], EXPOSURES).astype(jnp.int32),
    }


def psf_spectrum_full(stamp_set):
    placed = jnp.zeros((HEIGHT, WIDTH), jnp.float32).at[:STAMP, :STAMP].set(stamp_set)
    placed = jnp.roll(placed, (-(STAMP // 2), -(STAMP // 2)), axis=(0, 1))
    return jnp.fft.fft2(placed)[:, :WIDTH // 2]

def reference(exposures, stamps, zero_point, noise_var, footprint, accept, assign):
    half_width = WIDTH // 2
    accepted = accept.astype(jnp.float32)
    numer_weight = accepted * zero_point / noise_var
    denom_weight = accepted * zero_point * zero_point / noise_var
    row_ids = jnp.arange(HEIGHT, dtype=jnp.int32)
    numer_real = jnp.zeros((HEIGHT, half_width), jnp.float32)
    numer_imag = jnp.zeros((HEIGHT, half_width), jnp.float32)
    denom = jnp.zeros((HEIGHT, half_width), jnp.float32)
    for slot_no in range(EXPOSURES):
        exp_id = assign[slot_no]
        frame = exposures[slot_no]
        padded = jnp.pad(frame, 1)
        beside = padded[:-2, 1:-1] + padded[2:, 1:-1] + padded[1:-1, :-2] + padded[1:-1, 2:]
        inside = (row_ids >= footprint[exp_id, 0]) & (row_ids < footprint[exp_id, 1])
        cleaned = jnp.where(inside[:, None], frame - 0.25 * beside, 0.0)
        spectrum = jnp.fft.fft2(cleaned)[:, :half_width]
        kernel = psf_spectrum_full(stamps[exp_id])
        weight = numer_weight[exp_id]
        numer_real = numer_real + weight * (kernel.real * spectrum.real + kernel.imag * spectrum.imag)
        numer_imag = numer_imag + weight * (kernel.real * spectrum.imag - kernel.imag * spectrum.real)
        own_kernel = psf_spectrum_full(stamps[slot_no])
        denom = denom + denom_weight[slot_no] * (own_kernel.real * own_kernel.real + own_kernel.imag * own_kernel.imag)
    scale = 1.0 / math.sqrt(HEIGHT * WIDTH)
    root = jnp.sqrt(denom)
    return jnp.stack([numer_real / root * scale, numer_imag / root * scale])
```

```python
import functools
import math

import jax
import jax.numpy as jnp
import ml_dtypes
import numpy as np
from jax import lax
from jax.experimental import pallas as pl
from jax.experimental.pallas import tpu as pltpu
from jax.sharding import PartitionSpec as P

HIGHEST = lax.Precision.HIGHEST
TWO_PI = 2.0 * math.pi
HALO = 16
TILE = 128
BF16 = jnp.bfloat16
F32 = jnp.float32
READERS = ("read", "pair")


def split_np(table):
    hi = table.astype(np.float32).astype(ml_dtypes.bfloat16)
    lo = (table - hi.astype(np.float64)).astype(np.float32).astype(ml_dtypes.bfloat16)
    return hi, lo


def split(value):
    hi = value.astype(BF16)
    return hi, (value - hi.astype(F32)).astype(BF16)


def angles(left, right, modulus):
    return (np.outer(left, right) % modulus).astype(np.float64) * (TWO_PI / modulus)


def dot(left, right):
    return jnp.dot(left, right, preferred_element_type=F32)


def column_order(width, freqs, readers):
    share = width // 2 // freqs // readers
    parity = np.arange(2)[:, None, None, None]
    reader = np.arange(readers)[None, :, None, None]
    freq = np.arange(freqs)[None, None, :, None]
    inner = np.arange(share // 2)[None, None, None, :]
    ids = freq * (share * readers) + reader * share + 2 * inner + parity
    return ids.reshape(2, -1, TILE)


def row_tables(ids, width):
    half = np.arange(width // 2)
    parts = []
    for tile in range(ids.shape[1]):
        both = []
        for parity in range(2):
            phase = angles(half, ids[parity, tile], width)
            both.append(np.concatenate([np.cos(phase), -np.sin(phase)], axis=1))
        parts.append(np.stack(both))
    return split_np(np.stack(parts))


def front_kernel(info, low, block, high, taps, th, tl, out, ext, ch, cl, grid):
    rows, width = block.shape
    half = width // 2
    height = info[3]

    @pl.when(pl.program_id(0) == 0)
    def _():
        ext[:HALO] = low[...]
        ext[HALO : HALO + rows] = block[...]
        ext[HALO + rows :] = high[...]
        cols = lax.broadcasted_iota(jnp.int32, (16, width), 1)

        def clean(i, carry):
            at = pl.multiple_of(i * 16, 16)
            piece = ext[pl.ds(at, 32), :]
            mid = piece[8:24]
            ids = info[0] - 8 + at + lax.broadcasted_iota(jnp.int32, (16, 1), 0)
            ids = jnp.where(ids < 0, ids + height, ids)
            ids = jnp.where(ids >= height, ids - height, ids)
            up = jnp.where(ids == 0, 0.0, piece[7:23])
            down = jnp.where(ids == height - 1, 0.0, piece[9:25])
            left = jnp.where(cols == 0, 0.0, pltpu.roll(mid, 1, 1))
            right = jnp.where(cols == width - 1, 0.0, pltpu.roll(mid, width - 1, 1))
            inside = (ids >= info[1]) & (ids < info[2])
            cell = jnp.where(inside, mid - 0.25 * (up + down + left + right), 0.0)
            for parity in range(2):
                if parity == 0:
                    fold = cell[:, :half] + cell[:, half:]
                else:
                    fold = cell[:, :half] - cell[:, half:]
                hi, lo = split(fold)
                ch[parity, pl.ds(at, 16), :] = hi
                cl[parity, pl.ds(at, 16), :] = lo
            return carry

        lax.fori_loop(0, (rows + 16) // 16, clean, 0)

    for parity in range(2):
        grid[parity] = (
            dot(ch[parity], th[0, parity])
            + dot(ch[parity], tl[0, parity])
            + dot(cl[parity], th[0, parity])
        )

    def fir(i, carry):
        at = pl.multiple_of(i * 32, 32)
        for parity in range(2):
            re = grid[parity, pl.ds(at, 48), :TILE]
            im = grid[parity, pl.ds(at, 48), TILE:]
            sum_re = jnp.zeros((32, TILE), F32)
            sum_im = jnp.zeros((32, TILE), F32)
            for k in range(8):
                shift_re = re[k : k + 40]
                shift_im = im[k : k + 40]
                for a in (k, k + 8):
                    qr = taps[0, parity, 0, a : a + 1, :]
                    qi = taps[0, parity, 1, a : a + 1, :]
                    xr = shift_re[a - k : a - k + 32]
                    xi = shift_im[a - k : a - k + 32]
                    sum_re = sum_re + (qr * xr + qi * xi)
                    sum_im = sum_im + (qr * xi - qi * xr)
            lane = parity * 2 * TILE
            out[0, pl.ds(at, 32), lane : lane + TILE] = sum_re
            out[0, pl.ds(at, 32), lane + TILE : lane + 2 * TILE] = sum_im
        return carry

    lax.fori_loop(0, rows // 32, fir, 0)


def front(info, low, block, high, taps, tables):
    rows, width = block.shape
    tiles = tables[0].shape[0]
    whole = lambda shape: pl.BlockSpec(shape, lambda t: (0,) * len(shape))
    table_spec = pl.BlockSpec((1, 2, width // 2, 2 * TILE), lambda t: (t, 0, 0, 0))
    return pl.pallas_call(
        front_kernel,
        grid=(tiles,),
        out_shape=jax.ShapeDtypeStruct((tiles, rows, 4 * TILE), F32),
        in_specs=[
            pl.BlockSpec(memory_space=pltpu.SMEM),
            whole((HALO, width)),
            whole((rows, width)),
            whole((HALO, width)),
            pl.BlockSpec((1, 2, 2, taps.shape[3], TILE), lambda t: (t, 0, 0, 0, 0)),
            table_spec,
            table_spec,
        ],
        out_specs=pl.BlockSpec((1, rows, 4 * TILE), lambda t: (t, 0, 0)),
        scratch_shapes=[
            pltpu.VMEM((rows + 2 * HALO, width), F32),
            pltpu.VMEM((2, rows + 16, width // 2), BF16),
            pltpu.VMEM((2, rows + 16, width // 2), BF16),
            pltpu.VMEM((2, rows + 16, 2 * TILE), F32),
        ],
        compiler_params=pltpu.CompilerParams(vmem_limit_bytes=48 * 1024 * 1024),
        name="front",
    )(info, low, block, high, taps, *tables)


def column_tables(height):
    quarter = height // 4
    inner = np.arange(quarter)
    parts = []
    for j in range(4):
        phase = angles(4 * np.arange(quarter) + j, inner, height)
        parts.append(np.concatenate([np.cos(phase), np.sin(phase)], axis=1))
    return split_np(np.stack(parts))


def order_matrix(share):
    size = 2 * share
    table = np.zeros((size, 2 * size), np.float32)
    for part in range(2):
        for parity in range(2):
            for j in range(share // 2):
                source = part * share + parity * (share // 2) + j
                place = 2 * j + parity
                table[source, part * share + place] = 1.0
                table[source, size + (1 - part) * share + place] = -1.0 if part == 0 else 1.0
    return table.astype(ml_dtypes.bfloat16)


def column_kernel(x, order, th, tl, out):
    height, lanes = x.shape
    quarter = height // 4
    step = pl.program_id(0)
    for j in range(4):

        @pl.when(step == j)
        def _(j=j):
            parts = []
            for f in range(4):
                hi, lo = split(x[f * quarter : (f + 1) * quarter])
                parts.append(dot(hi, order[...]) + dot(lo, order[...]))
            if j % 2 == 0:
                even, odd = parts[0] + parts[2], parts[1] + parts[3]
                mix = even + odd if j == 0 else even - odd
                top, low = mix[:, :lanes], mix[:, lanes:]
            else:
                even, odd = parts[0] - parts[2], parts[1] - parts[3]
                sign = 1.0 if j == 1 else -1.0
                top = even[:, :lanes] + sign * odd[:, lanes:]
                low = even[:, lanes:] - sign * odd[:, :lanes]
            both = jnp.concatenate([top, low], axis=0)
            hi, lo = split(both)
            wide = dot(th[0], jnp.concatenate([hi, lo], axis=1))
            result = wide[:, :lanes] + wide[:, lanes:] + dot(tl[0], hi)
            out[pl.ds(j, quarter, stride=4), :] = result


def columns(x, order, tables):
    height, lanes = x.shape
    quarter = height // 4
    table_spec = pl.BlockSpec((1, quarter, 2 * quarter), lambda j: (j, 0, 0))
    return pl.pallas_call(
        column_kernel,
        grid=(4,),
        out_shape=jax.ShapeDtypeStruct((height, lanes), F32),
        in_specs=[
            pl.BlockSpec((height, lanes), lambda j: (0, 0)),
            pl.BlockSpec((lanes, 2 * lanes), lambda j: (0, 0)),
            table_spec,
            table_spec,
        ],
        out_specs=pl.BlockSpec((height, lanes), lambda j: (0, 0)),
        compiler_params=pltpu.CompilerParams(vmem_limit_bytes=48 * 1024 * 1024),
        name="columns",
    )(x, order, *tables)


def denom_kernel(weight, rows, cols, out):
    count = cols.shape[0]
    lanes = out.shape[1]
    total = jnp.zeros(out.shape, F32)
    rh, rl = split(rows[...])
    for e in range(count):
        chh, cll = split(cols[e])
        psf = dot(rh, chh) + dot(rh, cll) + dot(rl, chh)
        total = total + weight[e] * (psf[:, :lanes] * psf[:, :lanes] + psf[:, lanes:] * psf[:, lanes:])
    out[...] = lax.rsqrt(total)


def per_device(exposures, stamps, zero_point, noise_var, footprint, accept, assign):
    exp_dev, rows_dev, width = exposures.shape
    freqs = lax.axis_size("freq")
    readers = lax.axis_size(READERS)
    height = rows_dev * freqs
    per_freq = width // 2 // freqs
    share = per_freq // readers
    out_rows = height // readers
    stamp_len = stamps.shape[1]
    count_all = assign.shape[0]
    freq_at = lax.axis_index("freq")
    reader_at = lax.axis_index(READERS)
    ids = column_order(width, freqs, readers)
    tiles = ids.shape[1]
    offsets = np.arange(stamp_len) - stamp_len // 2

    block = exposures[0]
    forward = [(i, (i + 1) % freqs) for i in range(freqs)]
    backward = [(t, s) for s, t in forward]
    low = lax.ppermute(block[rows_dev - HALO :], "freq", forward)
    high = lax.ppermute(block[:HALO], "freq", backward)

    labels = jnp.arange(count_all, dtype=jnp.int32)
    owner = jnp.sum(jnp.where(labels == reader_at, assign, 0))
    chosen = labels == owner
    low_row = jnp.sum(jnp.where(chosen, footprint[:, 0], 0))
    high_row = jnp.sum(jnp.where(chosen, footprint[:, 1], 0))
    accepted = accept.astype(F32)
    numer_weight = accepted * zero_point / noise_var
    denom_weight = accepted * zero_point * zero_point / noise_var
    scale = 1.0 / math.sqrt(height * width)
    weight = jnp.sum(jnp.where(chosen, numer_weight, 0.0)) * scale
    stamp = jnp.sum(jnp.where(chosen[:, None, None], stamps, 0.0), axis=0) * weight
    tap_phase = angles(offsets, ids.reshape(-1), width)
    tap_table = np.stack([np.cos(tap_phase), -np.sin(tap_phase)]).astype(np.float32)
    taps = jnp.einsum("ab,cbp->cap", stamp, tap_table, precision=HIGHEST)
    taps = taps.reshape(2, stamp_len, 2, tiles, TILE).transpose(3, 2, 0, 1, 4)
    info = jnp.stack([freq_at * rows_dev, low_row, high_row, jnp.int32(height)]).astype(jnp.int32)

    terms = front(info, low, block, high, taps, row_tables(ids, width))
    if tiles != readers:
        terms = terms.reshape(tiles, rows_dev, 2, 2, readers // tiles, TILE * tiles // readers)
        terms = terms.transpose(0, 4, 1, 2, 3, 5).reshape(readers, rows_dev, -1)
    summed = lax.psum_scatter(terms, READERS, scatter_dimension=0, tiled=True)
    summed = summed.reshape(rows_dev, 2, 2, freqs, share // 2)
    summed = summed.transpose(3, 0, 2, 1, 4).reshape(freqs, rows_dev, 2 * share)
    gathered = lax.all_to_all(summed, "freq", split_axis=0, concat_axis=0, tiled=True)
    grid = columns(gathered.reshape(height, 2 * share), order_matrix(share), column_tables(height))
    grid = lax.all_to_all(
        grid.reshape(readers, out_rows, 2 * share), READERS, split_axis=0, concat_axis=0, tiled=True
    )
    numer = grid.reshape(readers, out_rows, 2, share).transpose(2, 1, 0, 3)
    numer = numer.reshape(2, out_rows, per_freq)

    all_u = angles(np.arange(height), offsets, height)
    all_rows = np.concatenate([np.cos(all_u), np.sin(all_u)], axis=1).astype(np.float32)
    psf_rows = lax.dynamic_slice_in_dim(jnp.asarray(all_rows), reader_at * out_rows, out_rows, 0)
    all_v = angles(offsets, np.arange(width // 2), width)
    all_cols = np.stack([np.cos(all_v), -np.sin(all_v)]).astype(np.float32)
    own_cols = lax.dynamic_slice_in_dim(jnp.asarray(all_cols), freq_at * per_freq, per_freq, 2)
    q = jnp.einsum("nab,cbp->cnap", stamps, own_cols, precision=HIGHEST)
    psf_cols = jnp.concatenate(
        [jnp.concatenate([q[0], q[1]], axis=2), jnp.concatenate([q[1], -q[0]], axis=2)], axis=1
    )
    inverse = pl.pallas_call(
        denom_kernel,
        out_shape=jax.ShapeDtypeStruct((out_rows, per_freq), F32),
        in_specs=[
            pl.BlockSpec(memory_space=pltpu.SMEM),
            pl.BlockSpec(memory_space=pltpu.VMEM),
            pl.BlockSpec(memory_space=pltpu.VMEM),
        ],
        out_specs=pl.BlockSpec(memory_space=pltpu.VMEM),
        compiler_params=pltpu.CompilerParams(vmem_limit_bytes=32 * 1024 * 1024),
        name="denom",
    )(denom_weight, psf_rows, psf_cols)
    return numer * inverse


def solution(mesh):
    in_specs = (
        P(("groups", "read", "pair"), "freq", None),
        P("groups", None, None),
        P("groups"),
        P("groups"),
        P("groups", None),
        P("groups"),
        P("groups"),
    )
    out_specs = P(None, ("groups", "read", "pair"), "freq")
    return jax.shard_map(
        per_device, mesh=mesh, in_specs=in_specs, out_specs=out_specs, check_vma=False
    )
```

```python
import functools
import math

import jax
import jax.numpy as jnp
import ml_dtypes
import numpy as np
from jax import lax
from jax.experimental import pallas as pl
from jax.experimental.pallas import tpu as pltpu
from jax.sharding import PartitionSpec as P

HIGHEST = lax.Precision.HIGHEST
TWO_PI = 2.0 * math.pi
HALO = 16
TILE = 128
BF16 = jnp.bfloat16
F32 = jnp.float32
READERS = ("read", "pair")


def split_np(table):
    hi = table.astype(np.float32).astype(ml_dtypes.bfloat16)
    lo = (table - hi.astype(np.float64)).astype(np.float32).astype(ml_dtypes.bfloat16)
    return hi, lo


def split(value):
    hi = value.astype(BF16)
    return hi, (value - hi.astype(F32)).astype(BF16)


def angles(left, right, modulus):
    return (np.outer(left, right) % modulus).astype(np.float64) * (TWO_PI / modulus)


def dot(left, right):
    return jnp.dot(left, right, preferred_element_type=F32)


def column_order(width, freqs, readers):
    share = width // 2 // freqs // readers
    parity = np.arange(2)[:, None, None, None]
    reader = np.arange(readers)[None, :, None, None]
    freq = np.arange(freqs)[None, None, :, None]
    inner = np.arange(share // 2)[None, None, None, :]
    ids = freq * (share * readers) + reader * share + 2 * inner + parity
    return ids.reshape(2, -1, TILE)


def row_tables(ids, width):
    half = np.arange(width // 2)
    parts = []
    for tile in range(ids.shape[1]):
        both = []
        for parity in range(2):
            phase = angles(half, ids[parity, tile], width)
            both.append(np.concatenate([np.cos(phase), -np.sin(phase)], axis=1))
        parts.append(np.stack(both))
    return split_np(np.stack(parts))


def front_kernel(info, low, block, high, taps, th, tl, out, ext, ch, cl, grid):
    rows, width = block.shape
    half = width // 2
    height = info[3]

    @pl.when(pl.program_id(0) == 0)
    def _():
        ext[:HALO] = low[...]
        ext[HALO : HALO + rows] = block[...]
        ext[HALO + rows :] = high[...]
        cols = lax.broadcasted_iota(jnp.int32, (16, width), 1)

        def clean(i, carry):
            at = pl.multiple_of(i * 16, 16)
            piece = ext[pl.ds(at, 32), :]
            mid = piece[8:24]
            ids = info[0] - 8 + at + lax.broadcasted_iota(jnp.int32, (16, 1), 0)
            ids = jnp.where(ids < 0, ids + height, ids)
            ids = jnp.where(ids >= height, ids - height, ids)
            up = jnp.where(ids == 0, 0.0, piece[7:23])
            down = jnp.where(ids == height - 1, 0.0, piece[9:25])
            left = jnp.where(cols == 0, 0.0, pltpu.roll(mid, 1, 1))
            right = jnp.where(cols == width - 1, 0.0, pltpu.roll(mid, width - 1, 1))
            inside = (ids >= info[1]) & (ids < info[2])
            cell = jnp.where(inside, mid - 0.25 * (up + down + left + right), 0.0)
            for parity in range(2):
                if parity == 0:
                    fold = cell[:, :half] + cell[:, half:]
                else:
                    fold = cell[:, :half] - cell[:, half:]
                hi, lo = split(fold)
                ch[parity, pl.ds(at, 16), :] = hi
                cl[parity, pl.ds(at, 16), :] = lo
            return carry

        lax.fori_loop(0, (rows + 16) // 16, clean, 0)

    for parity in range(2):
        grid[parity] = (
            dot(ch[parity], th[0, parity])
            + dot(ch[parity], tl[0, parity])
            + dot(cl[parity], th[0, parity])
        )

    def fir(i, carry):
        at = pl.multiple_of(i * 32, 32)
        for parity in range(2):
            re = grid[parity, pl.ds(at, 48), :TILE]
            im = grid[parity, pl.ds(at, 48), TILE:]
            sum_re = jnp.zeros((32, TILE), F32)
            sum_im = jnp.zeros((32, TILE), F32)
            for k in range(8):
                shift_re = re[k : k + 40]
                shift_im = im[k : k + 40]
                for a in (k, k + 8):
                    qr = taps[0, parity, 0, a : a + 1, :]
                    qi = taps[0, parity, 1, a : a + 1, :]
                    xr = shift_re[a - k : a - k + 32]
                    xi = shift_im[a - k : a - k + 32]
                    sum_re = sum_re + (qr * xr + qi * xi)
                    sum_im = sum_im + (qr * xi - qi * xr)
            lane = parity * 2 * TILE
            out[0, pl.ds(at, 32), lane : lane + TILE] = sum_re
            out[0, pl.ds(at, 32), lane + TILE : lane + 2 * TILE] = sum_im
        return carry

    lax.fori_loop(0, rows // 32, fir, 0)


def front(info, low, block, high, taps, tables):
    rows, width = block.shape
    tiles = tables[0].shape[0]
    whole = lambda shape: pl.BlockSpec(shape, lambda t: (0,) * len(shape))
    table_spec = pl.BlockSpec((1, 2, width // 2, 2 * TILE), lambda t: (t, 0, 0, 0))
    return pl.pallas_call(
        front_kernel,
        grid=(tiles,),
        out_shape=jax.ShapeDtypeStruct((tiles, rows, 4 * TILE), F32),
        in_specs=[
            pl.BlockSpec(memory_space=pltpu.SMEM),
            whole((HALO, width)),
            whole((rows, width)),
            whole((HALO, width)),
            pl.BlockSpec((1, 2, 2, taps.shape[3], TILE), lambda t: (t, 0, 0, 0, 0)),
            table_spec,
            table_spec,
        ],
        out_specs=pl.BlockSpec((1, rows, 4 * TILE), lambda t: (t, 0, 0)),
        scratch_shapes=[
            pltpu.VMEM((rows + 2 * HALO, width), F32),
            pltpu.VMEM((2, rows + 16, width // 2), BF16),
            pltpu.VMEM((2, rows + 16, width // 2), BF16),
            pltpu.VMEM((2, rows + 16, 2 * TILE), F32),
        ],
        compiler_params=pltpu.CompilerParams(vmem_limit_bytes=48 * 1024 * 1024),
        name="front",
    )(info, low, block, high, taps, *tables)


CHUNKS = 4
MESH = pl.DeviceIdType.MESH


def clean_rows(info, low, block, high, ext, ch, cl, height):
    rows, width = block.shape
    half = width // 2
    ext[:HALO] = low[...]
    ext[HALO : HALO + rows] = block[...]
    ext[HALO + rows :] = high[...]
    cols = lax.broadcasted_iota(jnp.int32, (16, width), 1)

    def clean(i, carry):
        at = pl.multiple_of(i * 16, 16)
        piece = ext[pl.ds(at, 32), :]
        mid = piece[8:24]
        ids = info[0] - 8 + at + lax.broadcasted_iota(jnp.int32, (16, 1), 0)
        ids = jnp.where(ids < 0, ids + height, ids)
        ids = jnp.where(ids >= height, ids - height, ids)
        up = jnp.where(ids == 0, 0.0, piece[7:23])
        down = jnp.where(ids == height - 1, 0.0, piece[9:25])
        left = jnp.where(cols == 0, 0.0, pltpu.roll(mid, 1, 1))
        right = jnp.where(cols == width - 1, 0.0, pltpu.roll(mid, width - 1, 1))
        inside = (ids >= info[1]) & (ids < info[2])
        cell = jnp.where(inside, mid - 0.25 * (up + down + left + right), 0.0)
        for parity in range(2):
            if parity == 0:
                fold = cell[:, :half] + cell[:, half:]
            else:
                fold = cell[:, :half] - cell[:, half:]
            hi, lo = split(fold)
            ch[parity, pl.ds(at, 16), :] = hi
            cl[parity, pl.ds(at, 16), :] = lo
        return carry

    lax.fori_loop(0, (rows + 16) // 16, clean, 0)


def fused_kernel(
    freqs, info, low, block, high, taps, th, tl, out,
    ext, ch, cl, grid, bufh, bufl, work, pair_in, read_in, freq_out, freq_in,
    table_sem, pair_send, pair_recv, read_send, read_recv, freq_send, freq_recv,
):
    rows, width = block.shape
    height = rows * freqs
    chunk = rows // CHUNKS
    share = TILE // freqs
    r = lax.axis_index("read")
    p = lax.axis_index("pair")
    f = lax.axis_index("freq")

    def tile_at(s):
        rd = jnp.where(s < 2, 1 - r, r)
        pd = jnp.where(s % 2 == 0, 1 - p, p)
        return rd * 2 + pd

    def table_copies(s):
        t = tile_at(s)
        return (
            pltpu.make_async_copy(th.at[t], bufh.at[s], table_sem.at[0, s]),
            pltpu.make_async_copy(tl.at[t], bufl.at[s], table_sem.at[1, s]),
        )

    def pair_copy(n):
        return pltpu.make_async_remote_copy(
            src_ref=work.at[2 * n], dst_ref=pair_in.at[n],
            send_sem=pair_send.at[n], recv_sem=pair_recv.at[n],
            device_id={"pair": 1 - p}, device_id_type=MESH,
        )

    def read_copy(c):
        part = pl.ds(c * chunk, chunk)
        return pltpu.make_async_remote_copy(
            src_ref=work.at[1, part], dst_ref=read_in.at[part],
            send_sem=read_send.at[c], recv_sem=read_recv.at[c],
            device_id={"read": 1 - r}, device_id_type=MESH,
        )

    def freq_copy(d, c):
        part = pl.ds(c * chunk, chunk)
        to = lax.rem(f + d, freqs)
        return pltpu.make_async_remote_copy(
            src_ref=freq_out.at[to, part], dst_ref=freq_in.at[f, part],
            send_sem=freq_send.at[d - 1, c], recv_sem=freq_recv.at[d - 1, c],
            device_id={"freq": to}, device_id_type=MESH,
        )

    for s in range(4):
        for copy in table_copies(s):
            copy.start()
    barrier = pltpu.get_barrier_semaphore()
    pl.semaphore_signal(barrier, inc=1, device_id={"pair": 1 - p}, device_id_type=MESH)
    pl.semaphore_signal(barrier, inc=1, device_id={"read": 1 - r}, device_id_type=MESH)
    for d in range(1, freqs):
        pl.semaphore_signal(
            barrier, inc=1, device_id={"freq": lax.rem(f + d, freqs)}, device_id_type=MESH
        )
    clean_rows(info, low, block, high, ext, ch, cl, height)
    pl.semaphore_wait(barrier, freqs + 1)

    def step(s, carry):
        for copy in table_copies(s):
            copy.wait()
        t = tile_at(s)
        for parity in range(2):
            grid[parity] = (
                dot(ch[parity], bufh[s, parity])
                + dot(ch[parity], bufl[s, parity])
                + dot(cl[parity], bufh[s, parity])
            )

        def fir(i, inner):
            at = pl.multiple_of(i * 32, 32)
            for parity in range(2):
                re = grid[parity, pl.ds(at, 48), :TILE]
                im = grid[parity, pl.ds(at, 48), TILE:]
                sum_re = jnp.zeros((32, TILE), F32)
                sum_im = jnp.zeros((32, TILE), F32)
                for k in range(8):
                    shift_re = re[k : k + 40]
                    shift_im = im[k : k + 40]
                    for a in (k, k + 8):
                        qr = taps[t, parity, 0, a : a + 1, :]
                        qi = taps[t, parity, 1, a : a + 1, :]
                        xr = shift_re[a - k : a - k + 32]
                        xi = shift_im[a - k : a - k + 32]
                        sum_re = sum_re + (qr * xr + qi * xi)
                        sum_im = sum_im + (qr * xi - qi * xr)
                lane = parity * 2 * TILE
                work[s, pl.ds(at, 32), lane : lane + TILE] = sum_re
                work[s, pl.ds(at, 32), lane + TILE : lane + 2 * TILE] = sum_im
            return inner

        lax.fori_loop(0, rows // 32, fir, 0)

        @pl.when(s == 0)
        def _():
            pair_copy(0).start()

        @pl.when(s == 1)
        def _():
            pair_copy(0).wait_recv()
            for c in range(CHUNKS):
                part = pl.ds(c * chunk, chunk)
                work[1, part, :] = work[1, part, :] + pair_in[0, part, :]
                read_copy(c).start()

        @pl.when(s == 2)
        def _():
            pair_copy(1).start()

        return carry

    lax.fori_loop(0, 4, step, 0)

    pair_copy(1).wait_recv()
    lanes = lax.broadcasted_iota(jnp.int32, (32, TILE), 1) // share
    for c in range(CHUNKS):
        read_copy(c).wait_recv()

        def pack(i, carry, c=c):
            part = pl.ds(pl.multiple_of(c * chunk + i * 32, 32), 32)
            total = work[3, part, :] + pair_in[1, part, :] + read_in[part, :]
            quads = [
                total[:, q * TILE : (q + 1) * TILE]
                for q in (0, 2, 1, 3)
            ]
            for to in range(freqs):
                result = None
                for q in range(4):
                    shift = (q - to) * share % TILE
                    moved = quads[q] if shift == 0 else pltpu.roll(quads[q], shift, 1)
                    result = moved if q == 0 else jnp.where(lanes == q, moved, result)
                freq_out[to, part, :] = result
            return carry

        lax.fori_loop(0, chunk // 32, pack, 0)
        for d in range(1, freqs):
            freq_copy(d, c).start()
    out[f] = freq_out[f]
    for n in range(2):
        pair_copy(n).wait_send()
    for c in range(CHUNKS):
        read_copy(c).wait_send()
    for d in range(1, freqs):
        for c in range(CHUNKS):
            freq_copy(d, c).wait()
        source = lax.rem(f + freqs - d, freqs)
        out[source] = freq_in[source]


def fused(info, low, block, high, taps, tables, freqs):
    rows, width = block.shape
    half = width // 2
    vmem = pl.BlockSpec(memory_space=pltpu.VMEM)
    anywhere = pl.BlockSpec(memory_space=pl.ANY)
    dma = pltpu.SemaphoreType.DMA
    return pl.pallas_call(
        functools.partial(fused_kernel, freqs),
        out_shape=jax.ShapeDtypeStruct((freqs, rows, TILE), F32),
        in_specs=[pl.BlockSpec(memory_space=pltpu.SMEM), vmem, vmem, vmem, vmem, anywhere, anywhere],
        out_specs=vmem,
        scratch_shapes=[
            pltpu.VMEM((rows + 2 * HALO, width), F32),
            pltpu.VMEM((2, rows + 16, half), BF16),
            pltpu.VMEM((2, rows + 16, half), BF16),
            pltpu.VMEM((2, rows + 16, 2 * TILE), F32),
            pltpu.VMEM((4, 2, half, 2 * TILE), BF16),
            pltpu.VMEM((4, 2, half, 2 * TILE), BF16),
            pltpu.VMEM((4, rows, 4 * TILE), F32),
            pltpu.VMEM((2, rows, 4 * TILE), F32),
            pltpu.VMEM((rows, 4 * TILE), F32),
            pltpu.VMEM((freqs, rows, TILE), F32),
            pltpu.VMEM((freqs, rows, TILE), F32),
            dma((2, 4)),
            dma((2,)),
            dma((2,)),
            dma((CHUNKS,)),
            dma((CHUNKS,)),
            dma((freqs - 1, CHUNKS)),
            dma((freqs - 1, CHUNKS)),
        ],
        compiler_params=pltpu.CompilerParams(
            collective_id=0, has_side_effects=True, vmem_limit_bytes=56 * 1024 * 1024
        ),
        cost_estimate=pl.CostEstimate(flops=7 * 10**9, bytes_accessed=14 * 2**20, transcendentals=0),
        name="fused",
    )(info, low, block, high, taps, *tables)


def column_tables(height):
    quarter = height // 4
    inner = np.arange(quarter)
    parts = []
    for j in range(4):
        phase = angles(4 * np.arange(quarter) + j, inner, height)
        parts.append(np.concatenate([np.cos(phase), np.sin(phase)], axis=1))
    return split_np(np.stack(parts))


def order_matrix(share):
    size = 2 * share
    table = np.zeros((size, 2 * size), np.float32)
    for part in range(2):
        for parity in range(2):
            for j in range(share // 2):
                source = part * share + parity * (share // 2) + j
                place = 2 * j + parity
                table[source, part * share + place] = 1.0
                table[source, size + (1 - part) * share + place] = -1.0 if part == 0 else 1.0
    return table.astype(ml_dtypes.bfloat16)


def column_kernel(x, order, th, tl, out):
    height, lanes = x.shape
    quarter = height // 4
    step = pl.program_id(0)
    for j in range(4):

        @pl.when(step == j)
        def _(j=j):
            parts = []
            for f in range(4):
                hi, lo = split(x[f * quarter : (f + 1) * quarter])
                parts.append(dot(hi, order[...]) + dot(lo, order[...]))
            if j % 2 == 0:
                even, odd = parts[0] + parts[2], parts[1] + parts[3]
                mix = even + odd if j == 0 else even - odd
                top, low = mix[:, :lanes], mix[:, lanes:]
            else:
                even, odd = parts[0] - parts[2], parts[1] - parts[3]
                sign = 1.0 if j == 1 else -1.0
                top = even[:, :lanes] + sign * odd[:, lanes:]
                low = even[:, lanes:] - sign * odd[:, :lanes]
            both = jnp.concatenate([top, low], axis=0)
            hi, lo = split(both)
            wide = dot(th[0], jnp.concatenate([hi, lo], axis=1))
            result = wide[:, :lanes] + wide[:, lanes:] + dot(tl[0], hi)
            out[pl.ds(j, quarter, stride=4), :] = result


def columns(x, order, tables):
    height, lanes = x.shape
    quarter = height // 4
    table_spec = pl.BlockSpec((1, quarter, 2 * quarter), lambda j: (j, 0, 0))
    return pl.pallas_call(
        column_kernel,
        grid=(4,),
        out_shape=jax.ShapeDtypeStruct((height, lanes), F32),
        in_specs=[
            pl.BlockSpec((height, lanes), lambda j: (0, 0)),
            pl.BlockSpec((lanes, 2 * lanes), lambda j: (0, 0)),
            table_spec,
            table_spec,
        ],
        out_specs=pl.BlockSpec((height, lanes), lambda j: (0, 0)),
        compiler_params=pltpu.CompilerParams(vmem_limit_bytes=48 * 1024 * 1024),
        name="columns",
    )(x, order, *tables)


def denom_kernel(weight, rows, cols, out):
    count = cols.shape[0]
    lanes = out.shape[1]
    total = jnp.zeros(out.shape, F32)
    rh, rl = split(rows[...])
    for e in range(count):
        chh, cll = split(cols[e])
        psf = dot(rh, chh) + dot(rh, cll) + dot(rl, chh)
        total = total + weight[e] * (psf[:, :lanes] * psf[:, :lanes] + psf[:, lanes:] * psf[:, lanes:])
    out[...] = lax.rsqrt(total)


def per_device(exposures, stamps, zero_point, noise_var, footprint, accept, assign):
    exp_dev, rows_dev, width = exposures.shape
    freqs = lax.axis_size("freq")
    readers = lax.axis_size(READERS)
    height = rows_dev * freqs
    per_freq = width // 2 // freqs
    share = per_freq // readers
    out_rows = height // readers
    stamp_len = stamps.shape[1]
    count_all = assign.shape[0]
    freq_at = lax.axis_index("freq")
    reader_at = lax.axis_index(READERS)
    ids = column_order(width, freqs, readers)
    tiles = ids.shape[1]
    offsets = np.arange(stamp_len) - stamp_len // 2

    block = exposures[0]
    forward = [(i, (i + 1) % freqs) for i in range(freqs)]
    backward = [(t, s) for s, t in forward]
    low = lax.ppermute(block[rows_dev - HALO :], "freq", forward)
    high = lax.ppermute(block[:HALO], "freq", backward)

    labels = jnp.arange(count_all, dtype=jnp.int32)
    owner = jnp.sum(jnp.where(labels == reader_at, assign, 0))
    chosen = labels == owner
    low_row = jnp.sum(jnp.where(chosen, footprint[:, 0], 0))
    high_row = jnp.sum(jnp.where(chosen, footprint[:, 1], 0))
    accepted = accept.astype(F32)
    numer_weight = accepted * zero_point / noise_var
    denom_weight = accepted * zero_point * zero_point / noise_var
    scale = 1.0 / math.sqrt(height * width)
    weight = jnp.sum(jnp.where(chosen, numer_weight, 0.0)) * scale
    stamp = jnp.sum(jnp.where(chosen[:, None, None], stamps, 0.0), axis=0) * weight
    tap_phase = angles(offsets, ids.reshape(-1), width)
    tap_table = np.stack([np.cos(tap_phase), -np.sin(tap_phase)]).astype(np.float32)
    taps = jnp.einsum("ab,cbp->cap", stamp, tap_table, precision=HIGHEST)
    taps = taps.reshape(2, stamp_len, 2, tiles, TILE).transpose(3, 2, 0, 1, 4)
    info = jnp.stack([freq_at * rows_dev, low_row, high_row, jnp.int32(height)]).astype(jnp.int32)

    tables = row_tables(ids, width)
    if lax.axis_size("read") == 2 and lax.axis_size("pair") == 2 and tiles == 4 and freqs == 4:
        gathered = fused(info, low, block, high, taps, tables, freqs)
    else:
        terms = front(info, low, block, high, taps, tables)
        if tiles != readers:
            terms = terms.reshape(tiles, rows_dev, 2, 2, readers // tiles, TILE * tiles // readers)
            terms = terms.transpose(0, 4, 1, 2, 3, 5).reshape(readers, rows_dev, -1)
        summed = lax.psum_scatter(terms, READERS, scatter_dimension=0, tiled=True)
        summed = summed.reshape(rows_dev, 2, 2, freqs, share // 2)
        summed = summed.transpose(3, 0, 2, 1, 4).reshape(freqs, rows_dev, 2 * share)
        gathered = lax.all_to_all(summed, "freq", split_axis=0, concat_axis=0, tiled=True)
    grid = columns(gathered.reshape(height, 2 * share), order_matrix(share), column_tables(height))
    grid = lax.all_to_all(
        grid.reshape(readers, out_rows, 2 * share), READERS, split_axis=0, concat_axis=0, tiled=True
    )
    numer = grid.reshape(readers, out_rows, 2, share).transpose(2, 1, 0, 3)
    numer = numer.reshape(2, out_rows, per_freq)

    all_u = angles(np.arange(height), offsets, height)
    all_rows = np.concatenate([np.cos(all_u), np.sin(all_u)], axis=1).astype(np.float32)
    psf_rows = lax.dynamic_slice_in_dim(jnp.asarray(all_rows), reader_at * out_rows, out_rows, 0)
    all_v = angles(offsets, np.arange(width // 2), width)
    all_cols = np.stack([np.cos(all_v), -np.sin(all_v)]).astype(np.float32)
    own_cols = lax.dynamic_slice_in_dim(jnp.asarray(all_cols), freq_at * per_freq, per_freq, 2)
    q = jnp.einsum("nab,cbp->cnap", stamps, own_cols, precision=HIGHEST)
    psf_cols = jnp.concatenate(
        [jnp.concatenate([q[0], q[1]], axis=2), jnp.concatenate([q[1], -q[0]], axis=2)], axis=1
    )
    inverse = pl.pallas_call(
        denom_kernel,
        out_shape=jax.ShapeDtypeStruct((out_rows, per_freq), F32),
        in_specs=[
            pl.BlockSpec(memory_space=pltpu.SMEM),
            pl.BlockSpec(memory_space=pltpu.VMEM),
            pl.BlockSpec(memory_space=pltpu.VMEM),
        ],
        out_specs=pl.BlockSpec(memory_space=pltpu.VMEM),
        compiler_params=pltpu.CompilerParams(vmem_limit_bytes=32 * 1024 * 1024),
        name="denom",
    )(denom_weight, psf_rows, psf_cols)
    return numer * inverse


def solution(mesh):
    in_specs = (
        P(("groups", "read", "pair"), "freq", None),
        P("groups", None, None),
        P("groups"),
        P("groups"),
        P("groups", None),
        P("groups"),
        P("groups"),
    )
    out_specs = P(None, ("groups", "read", "pair"), "freq")
    return jax.shard_map(
        per_device, mesh=mesh, in_specs=in_specs, out_specs=out_specs, check_vma=False
    )
```

```python
import functools
import math

import jax
import jax.numpy as jnp
import ml_dtypes
import numpy as np
from jax import lax
from jax.experimental import pallas as pl
from jax.experimental.pallas import tpu as pltpu
from jax.sharding import PartitionSpec as P

HIGHEST = lax.Precision.HIGHEST
TWO_PI = 2.0 * math.pi
HALO = 16
TILE = 128
BF16 = jnp.bfloat16
F32 = jnp.float32
READERS = ("read", "pair")


def split_np(table):
    hi = table.astype(np.float32).astype(ml_dtypes.bfloat16)
    lo = (table - hi.astype(np.float64)).astype(np.float32).astype(ml_dtypes.bfloat16)
    return hi, lo


def split(value):
    hi = value.astype(BF16)
    return hi, (value - hi.astype(F32)).astype(BF16)


def angles(left, right, modulus):
    return (np.outer(left, right) % modulus).astype(np.float64) * (TWO_PI / modulus)


def dot(left, right):
    return jnp.dot(left, right, preferred_element_type=F32)


def column_order(width, freqs, readers):
    share = width // 2 // freqs // readers
    parity = np.arange(2)[:, None, None, None]
    reader = np.arange(readers)[None, :, None, None]
    freq = np.arange(freqs)[None, None, :, None]
    inner = np.arange(share // 2)[None, None, None, :]
    ids = freq * (share * readers) + reader * share + 2 * inner + parity
    return ids.reshape(2, -1, TILE)


def row_tables(ids, width):
    half = np.arange(width // 2)
    parts = []
    for tile in range(ids.shape[1]):
        both = []
        for parity in range(2):
            phase = angles(half, ids[parity, tile], width)
            both.append(np.concatenate([np.cos(phase), -np.sin(phase)], axis=1))
        parts.append(np.stack(both))
    return split_np(np.stack(parts))


def front_kernel(info, low, block, high, taps, th, tl, out, ext, ch, cl, grid):
    rows, width = block.shape
    half = width // 2
    height = info[3]

    @pl.when(pl.program_id(0) == 0)
    def _():
        ext[:HALO] = low[...]
        ext[HALO : HALO + rows] = block[...]
        ext[HALO + rows :] = high[...]
        cols = lax.broadcasted_iota(jnp.int32, (16, width), 1)

        def clean(i, carry):
            at = pl.multiple_of(i * 16, 16)
            piece = ext[pl.ds(at, 32), :]
            mid = piece[8:24]
            ids = info[0] - 8 + at + lax.broadcasted_iota(jnp.int32, (16, 1), 0)
            ids = jnp.where(ids < 0, ids + height, ids)
            ids = jnp.where(ids >= height, ids - height, ids)
            up = jnp.where(ids == 0, 0.0, piece[7:23])
            down = jnp.where(ids == height - 1, 0.0, piece[9:25])
            left = jnp.where(cols == 0, 0.0, pltpu.roll(mid, 1, 1))
            right = jnp.where(cols == width - 1, 0.0, pltpu.roll(mid, width - 1, 1))
            inside = (ids >= info[1]) & (ids < info[2])
            cell = jnp.where(inside, mid - 0.25 * (up + down + left + right), 0.0)
            for parity in range(2):
                if parity == 0:
                    fold = cell[:, :half] + cell[:, half:]
                else:
                    fold = cell[:, :half] - cell[:, half:]
                hi, lo = split(fold)
                ch[parity, pl.ds(at, 16), :] = hi
                cl[parity, pl.ds(at, 16), :] = lo
            return carry

        lax.fori_loop(0, (rows + 16) // 16, clean, 0)

    for parity in range(2):
        grid[parity] = (
            dot(ch[parity], th[0, parity])
            + dot(ch[parity], tl[0, parity])
            + dot(cl[parity], th[0, parity])
        )

    def fir(i, carry):
        at = pl.multiple_of(i * 32, 32)
        for parity in range(2):
            re = grid[parity, pl.ds(at, 48), :TILE]
            im = grid[parity, pl.ds(at, 48), TILE:]
            sum_re = jnp.zeros((32, TILE), F32)
            sum_im = jnp.zeros((32, TILE), F32)
            for k in range(8):
                shift_re = re[k : k + 40]
                shift_im = im[k : k + 40]
                for a in (k, k + 8):
                    qr = taps[0, parity, 0, a : a + 1, :]
                    qi = taps[0, parity, 1, a : a + 1, :]
                    xr = shift_re[a - k : a - k + 32]
                    xi = shift_im[a - k : a - k + 32]
                    sum_re = sum_re + (qr * xr + qi * xi)
                    sum_im = sum_im + (qr * xi - qi * xr)
            lane = parity * 2 * TILE
            out[0, pl.ds(at, 32), lane : lane + TILE] = sum_re
            out[0, pl.ds(at, 32), lane + TILE : lane + 2 * TILE] = sum_im
        return carry

    lax.fori_loop(0, rows // 32, fir, 0)


def front(info, low, block, high, taps, tables):
    rows, width = block.shape
    tiles = tables[0].shape[0]
    whole = lambda shape: pl.BlockSpec(shape, lambda t: (0,) * len(shape))
    table_spec = pl.BlockSpec((1, 2, width // 2, 2 * TILE), lambda t: (t, 0, 0, 0))
    return pl.pallas_call(
        front_kernel,
        grid=(tiles,),
        out_shape=jax.ShapeDtypeStruct((tiles, rows, 4 * TILE), F32),
        in_specs=[
            pl.BlockSpec(memory_space=pltpu.SMEM),
            whole((HALO, width)),
            whole((rows, width)),
            whole((HALO, width)),
            pl.BlockSpec((1, 2, 2, taps.shape[3], TILE), lambda t: (t, 0, 0, 0, 0)),
            table_spec,
            table_spec,
        ],
        out_specs=pl.BlockSpec((1, rows, 4 * TILE), lambda t: (t, 0, 0)),
        scratch_shapes=[
            pltpu.VMEM((rows + 2 * HALO, width), F32),
            pltpu.VMEM((2, rows + 16, width // 2), BF16),
            pltpu.VMEM((2, rows + 16, width // 2), BF16),
            pltpu.VMEM((2, rows + 16, 2 * TILE), F32),
        ],
        compiler_params=pltpu.CompilerParams(vmem_limit_bytes=48 * 1024 * 1024),
        name="front",
    )(info, low, block, high, taps, *tables)


CHUNKS = 4
MESH = pl.DeviceIdType.MESH


def fused_kernel(
    freqs, assign, footprint, accept, zero_point, noise_var,
    stamps, tap_table, psf_rows, psf_cols, order, block, th, tl, uh, ul, out,
    ext, ch, cl, grid, bufh, bufl, work, pair_in, read_in, freq_out, freq_in,
    taps, colh, coll, mixed, col_out, last_in, inverse,
    block_sem, table_sem, col_sem, halo_send, halo_recv, pair_send, pair_recv,
    read_send, read_recv, freq_send, freq_recv, last_send, last_recv,
):
    rows, width = block.shape
    half = width // 2
    height = rows * freqs
    chunk = rows // CHUNKS
    share = TILE // freqs
    count, stamp_len, _ = stamps.shape
    r = lax.axis_index("read")
    p = lax.axis_index("pair")
    f = lax.axis_index("freq")
    reader = r * 2 + p

    def tile_at(s):
        rd = jnp.where(s < 2, 1 - r, r)
        pd = jnp.where(s % 2 == 0, 1 - p, p)
        return rd * 2 + pd

    def table_copies(s):
        t = tile_at(s)
        return (
            pltpu.make_async_copy(th.at[t], bufh.at[s], table_sem.at[0, s]),
            pltpu.make_async_copy(tl.at[t], bufl.at[s], table_sem.at[1, s]),
        )

    col_copies = (
        pltpu.make_async_copy(uh, colh, col_sem.at[0]),
        pltpu.make_async_copy(ul, coll, col_sem.at[1]),
    )
    block_copy = pltpu.make_async_copy(block, ext.at[pl.ds(HALO, rows)], block_sem)

    def halo_copy(n):
        source = rows - HALO if n == 0 else 0
        place = 0 if n == 0 else HALO + rows
        to = lax.rem(f + (1 if n == 0 else freqs - 1), freqs)
        return pltpu.make_async_remote_copy(
            src_ref=block.at[pl.ds(source, HALO)], dst_ref=ext.at[pl.ds(place, HALO)],
            send_sem=halo_send.at[n], recv_sem=halo_recv.at[n],
            device_id={"freq": to}, device_id_type=MESH,
        )

    def pair_copy(n):
        return pltpu.make_async_remote_copy(
            src_ref=work.at[2 * n], dst_ref=pair_in.at[n],
            send_sem=pair_send.at[n], recv_sem=pair_recv.at[n],
            device_id={"pair": 1 - p}, device_id_type=MESH,
        )

    def read_copy(c):
        part = pl.ds(c * chunk, chunk)
        return pltpu.make_async_remote_copy(
            src_ref=work.at[1, part], dst_ref=read_in.at[part],
            send_sem=read_send.at[c], recv_sem=read_recv.at[c],
            device_id={"read": 1 - r}, device_id_type=MESH,
        )

    def freq_copy(d, c):
        part = pl.ds(c * chunk, chunk)
        to = lax.rem(f + d, freqs)
        return pltpu.make_async_remote_copy(
            src_ref=freq_out.at[to, part], dst_ref=freq_in.at[f, part],
            send_sem=freq_send.at[d - 1, c], recv_sem=freq_recv.at[d - 1, c],
            device_id={"freq": to}, device_id_type=MESH,
        )

    def last_copy(e, j):
        rd = r if e == 0 else 1 - r
        pd = p if e == 1 else 1 - p
        return pltpu.make_async_remote_copy(
            src_ref=col_out.at[j, pl.ds(pl.multiple_of((rd * 2 + pd) * TILE, TILE), TILE)],
            dst_ref=last_in.at[reader, j],
            send_sem=last_send.at[e, j], recv_sem=last_recv.at[e, j],
            device_id={"read": rd, "pair": pd}, device_id_type=MESH,
        )

    barrier = pltpu.get_barrier_semaphore()
    for to in (
        {"pair": 1 - p},
        {"read": 1 - r},
        {"read": 1 - r, "pair": 1 - p},
        *({"freq": lax.rem(f + d, freqs)} for d in range(1, freqs)),
    ):
        pl.semaphore_signal(barrier, inc=1, device_id=to, device_id_type=MESH)
    block_copy.start()
    for s in range(4):
        for copy in table_copies(s):
            copy.start()
    for copy in col_copies:
        copy.start()
    pl.semaphore_wait(barrier, freqs + 2)
    for n in range(2):
        halo_copy(n).start()

    owner = assign[reader]
    low_row = footprint[owner, 0]
    high_row = footprint[owner, 1]

    def spread(value):
        return jnp.full((1, 2 * TILE), value, F32)

    def gate(e):
        return spread(accept[e].astype(F32)) * spread(zero_point[e])

    weight = gate(owner) / spread(noise_var[owner]) * (1.0 / math.sqrt(height * width))
    all_taps = jnp.dot(stamps[owner], tap_table[...], precision=HIGHEST, preferred_element_type=F32)
    for part in range(2):
        for parity in range(2):
            for t in range(4):
                at = ((part * 2 + parity) * 4 + t) * TILE
                taps[t, parity, part] = all_taps[:, at : at + TILE] * weight[:, :TILE]

    block_copy.wait()
    cols = lax.broadcasted_iota(jnp.int32, (16, width), 1)

    def clean(i, carry):
        at = pl.multiple_of(i * 16, 16)
        piece = ext[pl.ds(at, 32), :]
        mid = piece[8:24]
        ids = f * rows - 8 + at + lax.broadcasted_iota(jnp.int32, (16, 1), 0)
        ids = jnp.where(ids < 0, ids + height, ids)
        ids = jnp.where(ids >= height, ids - height, ids)
        up = jnp.where(ids == 0, 0.0, piece[7:23])
        down = jnp.where(ids == height - 1, 0.0, piece[9:25])
        left = jnp.where(cols == 0, 0.0, pltpu.roll(mid, 1, 1))
        right = jnp.where(cols == width - 1, 0.0, pltpu.roll(mid, width - 1, 1))
        inside = (ids >= low_row) & (ids < high_row)
        cell = jnp.where(inside, mid - 0.25 * (up + down + left + right), 0.0)
        for parity in range(2):
            if parity == 0:
                fold = cell[:, :half] + cell[:, half:]
            else:
                fold = cell[:, :half] - cell[:, half:]
            hi, lo = split(fold)
            ch[parity, pl.ds(at, 16), :] = hi
            cl[parity, pl.ds(at, 16), :] = lo
        return carry

    lax.fori_loop(1, rows // 16, clean, 0)
    for n in range(2):
        halo_copy(n).wait()
    lax.fori_loop(0, 2, lambda n, carry: clean(n * (rows // 16), carry), 0)

    def step(s, carry):
        for copy in table_copies(s):
            copy.wait()
        t = tile_at(s)
        for parity in range(2):
            grid[parity] = (
                dot(ch[parity], bufh[s, parity])
                + dot(ch[parity], bufl[s, parity])
                + dot(cl[parity], bufh[s, parity])
            )

        def fir(i, inner):
            at = pl.multiple_of(i * 32, 32)
            for parity in range(2):
                re = grid[parity, pl.ds(at, 48), :TILE]
                im = grid[parity, pl.ds(at, 48), TILE:]
                sum_re = jnp.zeros((32, TILE), F32)
                sum_im = jnp.zeros((32, TILE), F32)
                for k in range(8):
                    shift_re = re[k : k + 40]
                    shift_im = im[k : k + 40]
                    for a in (k, k + 8):
                        qr = taps[t, parity, 0, a : a + 1, :]
                        qi = taps[t, parity, 1, a : a + 1, :]
                        xr = shift_re[a - k : a - k + 32]
                        xi = shift_im[a - k : a - k + 32]
                        sum_re = sum_re + (qr * xr + qi * xi)
                        sum_im = sum_im + (qr * xi - qi * xr)
                lane = parity * 2 * TILE
                work[s, pl.ds(at, 32), lane : lane + TILE] = sum_re
                work[s, pl.ds(at, 32), lane + TILE : lane + 2 * TILE] = sum_im
            return inner

        lax.fori_loop(0, rows // 32, fir, 0)

        @pl.when(s == 0)
        def _():
            pair_copy(0).start()

        @pl.when(s == 1)
        def _():
            pair_copy(0).wait_recv()
            for c in range(CHUNKS):
                part = pl.ds(c * chunk, chunk)
                work[1, part, :] = work[1, part, :] + pair_in[0, part, :]
                read_copy(c).start()

        @pl.when(s == 2)
        def _():
            pair_copy(1).start()

        return carry

    lax.fori_loop(0, 4, step, 0)

    pair_copy(1).wait_recv()
    lanes = lax.broadcasted_iota(jnp.int32, (32, TILE), 1) // share
    for c in range(CHUNKS):
        read_copy(c).wait_recv()

        def pack(i, carry, c=c):
            part = pl.ds(pl.multiple_of(c * chunk + i * 32, 32), 32)
            total = work[3, part, :] + pair_in[1, part, :] + read_in[part, :]
            quads = [total[:, q * TILE : (q + 1) * TILE] for q in (0, 2, 1, 3)]
            for to in range(freqs):
                result = None
                for q in range(4):
                    shift = (q - to) * share % TILE
                    moved = quads[q] if shift == 0 else pltpu.roll(quads[q], shift, 1)
                    result = moved if q == 0 else jnp.where(lanes == q, moved, result)
                freq_out[to, part, :] = result
            return carry

        lax.fori_loop(0, chunk // 32, pack, 0)
        for d in range(1, freqs):
            freq_copy(d, c).start()
    freq_in[f] = freq_out[f]

    wide = 2 * TILE
    q = jnp.dot(
        stamps[...].reshape(count * stamp_len, stamp_len), psf_cols[f],
        precision=HIGHEST, preferred_element_type=F32,
    )
    rh, rl = split(psf_rows[reader])
    total = jnp.zeros((rows, wide), F32)
    for e in range(count):
        q_re = q[e * stamp_len : (e + 1) * stamp_len, :wide]
        q_im = q[e * stamp_len : (e + 1) * stamp_len, wide:]
        both = jnp.concatenate(
            [jnp.concatenate([q_re, q_im], axis=1), jnp.concatenate([q_im, -q_re], axis=1)], axis=0
        )
        qh, ql = split(both)
        psf = dot(rh, qh) + dot(rh, ql) + dot(rl, qh)
        gain = gate(e) * spread(zero_point[e]) / spread(noise_var[e])
        total = total + gain * (psf[:, :wide] * psf[:, :wide] + psf[:, wide:] * psf[:, wide:])
    total = lax.rsqrt(total)
    for side in range(2):
        inverse[side] = total[:, side * TILE : (side + 1) * TILE]

    for c in range(CHUNKS):
        for d in range(1, freqs):
            freq_copy(d, c).wait_recv()
        parts = []
        for g in range(4):
            hi, lo = split(freq_in[g, pl.ds(c * chunk, chunk), :])
            parts.append(dot(hi, order[...]) + dot(lo, order[...]))
        for j in range(4):
            if j % 2 == 0:
                even, odd = parts[0] + parts[2], parts[1] + parts[3]
                mix = even + odd if j == 0 else even - odd
                top, low = mix[:, :TILE], mix[:, TILE:]
            else:
                even, odd = parts[0] - parts[2], parts[1] - parts[3]
                sign = 1.0 if j == 1 else -1.0
                top = even[:, :TILE] + sign * odd[:, TILE:]
                low = even[:, TILE:] - sign * odd[:, :TILE]
            for n, value in enumerate((top, low)):
                hi, lo = split(value)
                part = pl.ds(n * rows + c * chunk, chunk)
                mixed[j, part, :TILE] = hi
                mixed[j, part, TILE:] = lo
    for copy in col_copies:
        copy.wait()

    for j in range(4):
        both = dot(colh[j], mixed[j])
        col_out[j] = both[:, :TILE] + both[:, TILE:] + dot(coll[j], mixed[j, :, :TILE])
        for e in (1, 2, 0):
            last_copy(e, j).start()
    lanes = lax.broadcasted_iota(jnp.int32, (TILE, TILE), 1)
    for j in range(4):
        last_in[reader, j] = col_out[j, pl.ds(pl.multiple_of(reader * TILE, TILE), TILE), :]
        for e in range(3):
            last_copy(e, j).wait_recv()
        for side in range(2):
            one, two = last_in[2 * side, j], last_in[2 * side + 1, j]
            re = jnp.where(lanes < TILE // 2, one, pltpu.roll(two, TILE // 2, 1))
            im = jnp.where(lanes < TILE // 2, pltpu.roll(one, TILE // 2, 1), two)
            place = pl.ds(j, TILE, stride=4)
            gain = inverse[side, place, :]
            out[0, side, place, :] = re * gain
            out[1, side, place, :] = im * gain

    for n in range(2):
        pair_copy(n).wait_send()
    for c in range(CHUNKS):
        read_copy(c).wait_send()
        for d in range(1, freqs):
            freq_copy(d, c).wait_send()
    for e in range(3):
        for j in range(4):
            last_copy(e, j).wait_send()


def fused(scalars, stamps, ids, block, freqs, readers):
    rows, width = block.shape
    half = width // 2
    height = rows * freqs
    stamp_len = stamps.shape[1]
    offsets = np.arange(stamp_len) - stamp_len // 2
    phase = angles(offsets, ids.reshape(-1), width)
    tap_table = np.concatenate([np.cos(phase), -np.sin(phase)], axis=1).astype(np.float32)
    phase = angles(np.arange(height), offsets, height)
    psf_rows = np.concatenate([np.cos(phase), np.sin(phase)], axis=1).astype(np.float32)
    psf_rows = psf_rows.reshape(readers, height // readers, -1)
    phase = angles(offsets, np.arange(half), width).reshape(stamp_len, freqs, -1)
    psf_cols = np.concatenate([np.cos(phase), -np.sin(phase)], axis=2).astype(np.float32)
    psf_cols = psf_cols.transpose(1, 0, 2)
    order = order_matrix(TILE // 2)
    vmem = pl.BlockSpec(memory_space=pltpu.VMEM)
    smem = pl.BlockSpec(memory_space=pltpu.SMEM)
    anywhere = pl.BlockSpec(memory_space=pl.ANY)
    dma = pltpu.SemaphoreType.DMA
    result = pl.pallas_call(
        functools.partial(fused_kernel, freqs),
        out_shape=jax.ShapeDtypeStruct((2, 2, rows, TILE), F32),
        in_specs=[smem] * 5 + [vmem] * 5 + [anywhere] * 5,
        out_specs=vmem,
        scratch_shapes=[
            pltpu.VMEM((rows + 2 * HALO, width), F32),
            pltpu.VMEM((2, rows + 16, half), BF16),
            pltpu.VMEM((2, rows + 16, half), BF16),
            pltpu.VMEM((2, rows + 16, 2 * TILE), F32),
            pltpu.VMEM((4, 2, half, 2 * TILE), BF16),
            pltpu.VMEM((4, 2, half, 2 * TILE), BF16),
            pltpu.VMEM((4, rows, 4 * TILE), F32),
            pltpu.VMEM((2, rows, 4 * TILE), F32),
            pltpu.VMEM((rows, 4 * TILE), F32),
            pltpu.VMEM((freqs, rows, TILE), F32),
            pltpu.VMEM((freqs, rows, TILE), F32),
            pltpu.VMEM((4, 2, 2, stamp_len, TILE), F32),
            pltpu.VMEM((4, rows, 2 * rows), BF16),
            pltpu.VMEM((4, rows, 2 * rows), BF16),
            pltpu.VMEM((4, 2 * rows, 2 * TILE), BF16),
            pltpu.VMEM((4, rows, TILE), F32),
            pltpu.VMEM((4, 4, TILE, TILE), F32),
            pltpu.VMEM((2, rows, TILE), F32),
            dma,
            dma((2, 4)),
            dma((2,)),
            dma((2,)),
            dma((2,)),
            dma((2,)),
            dma((2,)),
            dma((CHUNKS,)),
            dma((CHUNKS,)),
            dma((freqs - 1, CHUNKS)),
            dma((freqs - 1, CHUNKS)),
            dma((3, 4)),
            dma((3, 4)),
        ],
        compiler_params=pltpu.CompilerParams(
            collective_id=0, has_side_effects=True, vmem_limit_bytes=58 * 1024 * 1024
        ),
        name="fused",
    )(
        *scalars, stamps, tap_table, psf_rows, psf_cols, order, block,
        *row_tables(ids, width), *column_tables(height),
    )
    return result.transpose(0, 2, 1, 3).reshape(2, rows, 2 * TILE)


def column_tables(height):
    quarter = height // 4
    inner = np.arange(quarter)
    parts = []
    for j in range(4):
        phase = angles(4 * np.arange(quarter) + j, inner, height)
        parts.append(np.concatenate([np.cos(phase), np.sin(phase)], axis=1))
    return split_np(np.stack(parts))


def order_matrix(share):
    size = 2 * share
    table = np.zeros((size, 2 * size), np.float32)
    for part in range(2):
        for parity in range(2):
            for j in range(share // 2):
                source = part * share + parity * (share // 2) + j
                place = 2 * j + parity
                table[source, part * share + place] = 1.0
                table[source, size + (1 - part) * share + place] = -1.0 if part == 0 else 1.0
    return table.astype(ml_dtypes.bfloat16)


def column_kernel(x, order, th, tl, out):
    height, lanes = x.shape
    quarter = height // 4
    step = pl.program_id(0)
    for j in range(4):

        @pl.when(step == j)
        def _(j=j):
            parts = []
            for f in range(4):
                hi, lo = split(x[f * quarter : (f + 1) * quarter])
                parts.append(dot(hi, order[...]) + dot(lo, order[...]))
            if j % 2 == 0:
                even, odd = parts[0] + parts[2], parts[1] + parts[3]
                mix = even + odd if j == 0 else even - odd
                top, low = mix[:, :lanes], mix[:, lanes:]
            else:
                even, odd = parts[0] - parts[2], parts[1] - parts[3]
                sign = 1.0 if j == 1 else -1.0
                top = even[:, :lanes] + sign * odd[:, lanes:]
                low = even[:, lanes:] - sign * odd[:, :lanes]
            both = jnp.concatenate([top, low], axis=0)
            hi, lo = split(both)
            wide = dot(th[0], jnp.concatenate([hi, lo], axis=1))
            result = wide[:, :lanes] + wide[:, lanes:] + dot(tl[0], hi)
            out[pl.ds(j, quarter, stride=4), :] = result


def columns(x, order, tables):
    height, lanes = x.shape
    quarter = height // 4
    table_spec = pl.BlockSpec((1, quarter, 2 * quarter), lambda j: (j, 0, 0))
    return pl.pallas_call(
        column_kernel,
        grid=(4,),
        out_shape=jax.ShapeDtypeStruct((height, lanes), F32),
        in_specs=[
            pl.BlockSpec((height, lanes), lambda j: (0, 0)),
            pl.BlockSpec((lanes, 2 * lanes), lambda j: (0, 0)),
            table_spec,
            table_spec,
        ],
        out_specs=pl.BlockSpec((height, lanes), lambda j: (0, 0)),
        compiler_params=pltpu.CompilerParams(vmem_limit_bytes=48 * 1024 * 1024),
        name="columns",
    )(x, order, *tables)


def denom_kernel(weight, rows, cols, out):
    count = cols.shape[0]
    lanes = out.shape[1]
    total = jnp.zeros(out.shape, F32)
    rh, rl = split(rows[...])
    for e in range(count):
        chh, cll = split(cols[e])
        psf = dot(rh, chh) + dot(rh, cll) + dot(rl, chh)
        total = total + weight[e] * (psf[:, :lanes] * psf[:, :lanes] + psf[:, lanes:] * psf[:, lanes:])
    out[...] = lax.rsqrt(total)


def per_device(exposures, stamps, zero_point, noise_var, footprint, accept, assign):
    exp_dev, rows_dev, width = exposures.shape
    freqs = lax.axis_size("freq")
    readers = lax.axis_size(READERS)
    height = rows_dev * freqs
    per_freq = width // 2 // freqs
    share = per_freq // readers
    out_rows = height // readers
    stamp_len = stamps.shape[1]
    count_all = assign.shape[0]
    freq_at = lax.axis_index("freq")
    reader_at = lax.axis_index(READERS)
    ids = column_order(width, freqs, readers)
    tiles = ids.shape[1]
    offsets = np.arange(stamp_len) - stamp_len // 2

    block = exposures[0]
    square = lax.axis_size("read") == 2 and lax.axis_size("pair") == 2
    if square and tiles == 4 and freqs == 4 and rows_dev == 4 * TILE:
        scalars = (assign, footprint, accept, zero_point, noise_var)
        return fused(scalars, stamps, ids, block, freqs, readers)
    forward = [(i, (i + 1) % freqs) for i in range(freqs)]
    backward = [(t, s) for s, t in forward]
    low = lax.ppermute(block[rows_dev - HALO :], "freq", forward)
    high = lax.ppermute(block[:HALO], "freq", backward)

    labels = jnp.arange(count_all, dtype=jnp.int32)
    owner = jnp.sum(jnp.where(labels == reader_at, assign, 0))
    chosen = labels == owner
    low_row = jnp.sum(jnp.where(chosen, footprint[:, 0], 0))
    high_row = jnp.sum(jnp.where(chosen, footprint[:, 1], 0))
    accepted = accept.astype(F32)
    numer_weight = accepted * zero_point / noise_var
    denom_weight = accepted * zero_point * zero_point / noise_var
    scale = 1.0 / math.sqrt(height * width)
    weight = jnp.sum(jnp.where(chosen, numer_weight, 0.0)) * scale
    stamp = jnp.sum(jnp.where(chosen[:, None, None], stamps, 0.0), axis=0) * weight
    tap_phase = angles(offsets, ids.reshape(-1), width)
    tap_table = np.stack([np.cos(tap_phase), -np.sin(tap_phase)]).astype(np.float32)
    taps = jnp.einsum("ab,cbp->cap", stamp, tap_table, precision=HIGHEST)
    taps = taps.reshape(2, stamp_len, 2, tiles, TILE).transpose(3, 2, 0, 1, 4)
    info = jnp.stack([freq_at * rows_dev, low_row, high_row, jnp.int32(height)]).astype(jnp.int32)

    tables = row_tables(ids, width)
    terms = front(info, low, block, high, taps, tables)
    if tiles != readers:
        terms = terms.reshape(tiles, rows_dev, 2, 2, readers // tiles, TILE * tiles // readers)
        terms = terms.transpose(0, 4, 1, 2, 3, 5).reshape(readers, rows_dev, -1)
    summed = lax.psum_scatter(terms, READERS, scatter_dimension=0, tiled=True)
    summed = summed.reshape(rows_dev, 2, 2, freqs, share // 2)
    summed = summed.transpose(3, 0, 2, 1, 4).reshape(freqs, rows_dev, 2 * share)
    gathered = lax.all_to_all(summed, "freq", split_axis=0, concat_axis=0, tiled=True)
    grid = columns(gathered.reshape(height, 2 * share), order_matrix(share), column_tables(height))
    grid = lax.all_to_all(
        grid.reshape(readers, out_rows, 2 * share), READERS, split_axis=0, concat_axis=0, tiled=True
    )
    numer = grid.reshape(readers, out_rows, 2, share).transpose(2, 1, 0, 3)
    numer = numer.reshape(2, out_rows, per_freq)

    all_u = angles(np.arange(height), offsets, height)
    all_rows = np.concatenate([np.cos(all_u), np.sin(all_u)], axis=1).astype(np.float32)
    psf_rows = lax.dynamic_slice_in_dim(jnp.asarray(all_rows), reader_at * out_rows, out_rows, 0)
    all_v = angles(offsets, np.arange(width // 2), width)
    all_cols = np.stack([np.cos(all_v), -np.sin(all_v)]).astype(np.float32)
    own_cols = lax.dynamic_slice_in_dim(jnp.asarray(all_cols), freq_at * per_freq, per_freq, 2)
    q = jnp.einsum("nab,cbp->cnap", stamps, own_cols, precision=HIGHEST)
    psf_cols = jnp.concatenate(
        [jnp.concatenate([q[0], q[1]], axis=2), jnp.concatenate([q[1], -q[0]], axis=2)], axis=1
    )
    inverse = pl.pallas_call(
        denom_kernel,
        out_shape=jax.ShapeDtypeStruct((out_rows, per_freq), F32),
        in_specs=[
            pl.BlockSpec(memory_space=pltpu.SMEM),
            pl.BlockSpec(memory_space=pltpu.VMEM),
            pl.BlockSpec(memory_space=pltpu.VMEM),
        ],
        out_specs=pl.BlockSpec(memory_space=pltpu.VMEM),
        compiler_params=pltpu.CompilerParams(vmem_limit_bytes=32 * 1024 * 1024),
        name="denom",
    )(denom_weight, psf_rows, psf_cols)
    return numer * inverse


def solution(mesh):
    in_specs = (
        P(("groups", "read", "pair"), "freq", None),
        P("groups", None, None),
        P("groups"),
        P("groups"),
        P("groups", None),
        P("groups"),
        P("groups"),
    )
    out_specs = P(None, ("groups", "read", "pair"), "freq")
    return jax.shard_map(
        per_device, mesh=mesh, in_specs=in_specs, out_specs=out_specs, check_vma=False
    )
```

```python
import functools
import math

import jax
import jax.numpy as jnp
import ml_dtypes
import numpy as np
from jax import lax
from jax.experimental import pallas as pl
from jax.experimental.pallas import tpu as pltpu
from jax.sharding import PartitionSpec as P

HIGHEST = lax.Precision.HIGHEST
TWO_PI = 2.0 * math.pi
HALO = 16
TILE = 128
BF16 = jnp.bfloat16
F32 = jnp.float32
READERS = ("read", "pair")


def split_np(table):
    hi = table.astype(np.float32).astype(ml_dtypes.bfloat16)
    lo = (table - hi.astype(np.float64)).astype(np.float32).astype(ml_dtypes.bfloat16)
    return hi, lo


def split(value):
    hi = value.astype(BF16)
    return hi, (value - hi.astype(F32)).astype(BF16)


def angles(left, right, modulus):
    return (np.outer(left, right) % modulus).astype(np.float64) * (TWO_PI / modulus)


def dot(left, right):
    return jnp.dot(left, right, preferred_element_type=F32)


def column_order(width, freqs, readers):
    share = width // 2 // freqs // readers
    parity = np.arange(2)[:, None, None, None]
    reader = np.arange(readers)[None, :, None, None]
    freq = np.arange(freqs)[None, None, :, None]
    inner = np.arange(share // 2)[None, None, None, :]
    ids = freq * (share * readers) + reader * share + 2 * inner + parity
    return ids.reshape(2, -1, TILE)


def row_tables(ids, width):
    half = np.arange(width // 2)
    parts = []
    for tile in range(ids.shape[1]):
        both = []
        for parity in range(2):
            phase = angles(half, ids[parity, tile], width)
            both.append(np.concatenate([np.cos(phase), -np.sin(phase)], axis=1))
        parts.append(np.stack(both))
    return split_np(np.stack(parts))


def front_kernel(info, low, block, high, taps, th, tl, out, ext, ch, cl, grid):
    rows, width = block.shape
    half = width // 2
    height = info[3]

    @pl.when(pl.program_id(0) == 0)
    def _():
        ext[:HALO] = low[...]
        ext[HALO : HALO + rows] = block[...]
        ext[HALO + rows :] = high[...]
        cols = lax.broadcasted_iota(jnp.int32, (16, width), 1)

        def clean(i, carry):
            at = pl.multiple_of(i * 16, 16)
            piece = ext[pl.ds(at, 32), :]
            mid = piece[8:24]
            ids = info[0] - 8 + at + lax.broadcasted_iota(jnp.int32, (16, 1), 0)
            ids = jnp.where(ids < 0, ids + height, ids)
            ids = jnp.where(ids >= height, ids - height, ids)
            up = jnp.where(ids == 0, 0.0, piece[7:23])
            down = jnp.where(ids == height - 1, 0.0, piece[9:25])
            left = jnp.where(cols == 0, 0.0, pltpu.roll(mid, 1, 1))
            right = jnp.where(cols == width - 1, 0.0, pltpu.roll(mid, width - 1, 1))
            inside = (ids >= info[1]) & (ids < info[2])
            cell = jnp.where(inside, mid - 0.25 * (up + down + left + right), 0.0)
            for parity in range(2):
                if parity == 0:
                    fold = cell[:, :half] + cell[:, half:]
                else:
                    fold = cell[:, :half] - cell[:, half:]
                hi, lo = split(fold)
                ch[parity, pl.ds(at, 16), :] = hi
                cl[parity, pl.ds(at, 16), :] = lo
            return carry

        lax.fori_loop(0, (rows + 16) // 16, clean, 0)

    for parity in range(2):
        grid[parity] = (
            dot(ch[parity], th[0, parity])
            + dot(ch[parity], tl[0, parity])
            + dot(cl[parity], th[0, parity])
        )

    def fir(i, carry):
        at = pl.multiple_of(i * 32, 32)
        for parity in range(2):
            re = grid[parity, pl.ds(at, 48), :TILE]
            im = grid[parity, pl.ds(at, 48), TILE:]
            sum_re = jnp.zeros((32, TILE), F32)
            sum_im = jnp.zeros((32, TILE), F32)
            for k in range(8):
                shift_re = re[k : k + 40]
                shift_im = im[k : k + 40]
                for a in (k, k + 8):
                    qr = taps[0, parity, 0, a : a + 1, :]
                    qi = taps[0, parity, 1, a : a + 1, :]
                    xr = shift_re[a - k : a - k + 32]
                    xi = shift_im[a - k : a - k + 32]
                    sum_re = sum_re + (qr * xr + qi * xi)
                    sum_im = sum_im + (qr * xi - qi * xr)
            lane = parity * 2 * TILE
            out[0, pl.ds(at, 32), lane : lane + TILE] = sum_re
            out[0, pl.ds(at, 32), lane + TILE : lane + 2 * TILE] = sum_im
        return carry

    lax.fori_loop(0, rows // 32, fir, 0)


def front(info, low, block, high, taps, tables):
    rows, width = block.shape
    tiles = tables[0].shape[0]
    whole = lambda shape: pl.BlockSpec(shape, lambda t: (0,) * len(shape))
    table_spec = pl.BlockSpec((1, 2, width // 2, 2 * TILE), lambda t: (t, 0, 0, 0))
    return pl.pallas_call(
        front_kernel,
        grid=(tiles,),
        out_shape=jax.ShapeDtypeStruct((tiles, rows, 4 * TILE), F32),
        in_specs=[
            pl.BlockSpec(memory_space=pltpu.SMEM),
            whole((HALO, width)),
            whole((rows, width)),
            whole((HALO, width)),
            pl.BlockSpec((1, 2, 2, taps.shape[3], TILE), lambda t: (t, 0, 0, 0, 0)),
            table_spec,
            table_spec,
        ],
        out_specs=pl.BlockSpec((1, rows, 4 * TILE), lambda t: (t, 0, 0)),
        scratch_shapes=[
            pltpu.VMEM((rows + 2 * HALO, width), F32),
            pltpu.VMEM((2, rows + 16, width // 2), BF16),
            pltpu.VMEM((2, rows + 16, width // 2), BF16),
            pltpu.VMEM((2, rows + 16, 2 * TILE), F32),
        ],
        compiler_params=pltpu.CompilerParams(vmem_limit_bytes=48 * 1024 * 1024),
        name="front",
    )(info, low, block, high, taps, *tables)


CHUNKS = 4
MESH = pl.DeviceIdType.MESH


def fused_kernel(
    freqs, assign, footprint, accept, zero_point, noise_var,
    stamps, tap_table, psf_rows, psf_cols, order, block, th, tl, uh, ul, out,
    ext, ch, cl, grid, bufh, bufl, work, pair_in, read_in, freq_out, freq_in,
    taps, colh, coll, stage, col_out, last_in, inverse,
    block_sem, table_sem, col_sem, halo_send, halo_recv, pair_send, pair_recv,
    read_send, read_recv, freq_send, freq_recv, last_send, last_recv,
):
    rows, width = block.shape
    half = width // 2
    height = rows * freqs
    chunk = rows // CHUNKS
    share = TILE // freqs
    count, stamp_len, _ = stamps.shape
    r = lax.axis_index("read")
    p = lax.axis_index("pair")
    f = lax.axis_index("freq")
    reader = r * 2 + p

    def tile_at(s):
        rd = jnp.where(s < 2, 1 - r, r)
        pd = jnp.where(s % 2 == 0, 1 - p, p)
        return rd * 2 + pd

    def table_copies(s):
        t = tile_at(s)
        return (
            pltpu.make_async_copy(th.at[t], bufh.at[s], table_sem.at[0, s]),
            pltpu.make_async_copy(tl.at[t], bufl.at[s], table_sem.at[1, s]),
        )

    col_copies = (
        pltpu.make_async_copy(uh, colh, col_sem.at[0]),
        pltpu.make_async_copy(ul, coll, col_sem.at[1]),
    )
    block_copy = pltpu.make_async_copy(block, ext.at[pl.ds(HALO, rows)], block_sem)

    def halo_copy(n):
        source = rows - HALO if n == 0 else 0
        place = 0 if n == 0 else HALO + rows
        to = lax.rem(f + (1 if n == 0 else freqs - 1), freqs)
        return pltpu.make_async_remote_copy(
            src_ref=block.at[pl.ds(source, HALO)], dst_ref=ext.at[pl.ds(place, HALO)],
            send_sem=halo_send.at[n], recv_sem=halo_recv.at[n],
            device_id={"freq": to}, device_id_type=MESH,
        )

    def pair_copy(n):
        return pltpu.make_async_remote_copy(
            src_ref=work.at[2 * n], dst_ref=pair_in.at[n],
            send_sem=pair_send.at[n], recv_sem=pair_recv.at[n],
            device_id={"pair": 1 - p}, device_id_type=MESH,
        )

    def read_copy(c):
        part = pl.ds(c * chunk, chunk)
        return pltpu.make_async_remote_copy(
            src_ref=work.at[1, part], dst_ref=read_in.at[part],
            send_sem=read_send.at[c], recv_sem=read_recv.at[c],
            device_id={"read": 1 - r}, device_id_type=MESH,
        )

    def freq_copy(d, c):
        part = pl.ds(c * chunk, chunk)
        to = lax.rem(f + d, freqs)
        return pltpu.make_async_remote_copy(
            src_ref=freq_out.at[to, part], dst_ref=freq_in.at[f, part],
            send_sem=freq_send.at[d - 1, c], recv_sem=freq_recv.at[d - 1, c],
            device_id={"freq": to}, device_id_type=MESH,
        )

    def last_copy(e, j):
        rd = r if e == 0 else 1 - r
        pd = p if e == 1 else 1 - p
        return pltpu.make_async_remote_copy(
            src_ref=col_out.at[j, pl.ds(pl.multiple_of((rd * 2 + pd) * TILE, TILE), TILE)],
            dst_ref=last_in.at[reader, j],
            send_sem=last_send.at[e, j], recv_sem=last_recv.at[e, j],
            device_id={"read": rd, "pair": pd}, device_id_type=MESH,
        )

    barrier = pltpu.get_barrier_semaphore()
    for to in (
        {"pair": 1 - p},
        {"read": 1 - r},
        {"read": 1 - r, "pair": 1 - p},
        *({"freq": lax.rem(f + d, freqs)} for d in range(1, freqs)),
    ):
        pl.semaphore_signal(barrier, inc=1, device_id=to, device_id_type=MESH)
    block_copy.start()
    for s in range(4):
        for copy in table_copies(s):
            copy.start()
    for copy in col_copies:
        copy.start()
    pl.semaphore_wait(barrier, freqs + 2)
    for n in range(2):
        halo_copy(n).start()

    owner = assign[reader]
    low_row = footprint[owner, 0]
    high_row = footprint[owner, 1]

    def spread(value):
        return jnp.full((1, 2 * TILE), value, F32)

    def gate(e):
        return spread(accept[e].astype(F32)) * spread(zero_point[e])

    weight = gate(owner) / spread(noise_var[owner]) * (1.0 / math.sqrt(height * width))
    all_taps = jnp.dot(stamps[owner], tap_table[...], precision=HIGHEST, preferred_element_type=F32)
    for parity in range(2):
        for t in range(4):
            at = (parity * 4 + t) * TILE
            re = all_taps[:, at : at + TILE] * weight[:, :TILE]
            im = all_taps[:, half + at : half + at + TILE] * weight[:, :TILE]
            taps[t, parity, 0] = re
            taps[t, parity, 1] = im - re
            taps[t, parity, 2] = im + re

    block_copy.wait()
    cols = lax.broadcasted_iota(jnp.int32, (16, width), 1)

    def clean(i, carry):
        at = pl.multiple_of(i * 16, 16)
        piece = ext[pl.ds(at, 32), :]
        mid = piece[8:24]
        ids = f * rows - 8 + at + lax.broadcasted_iota(jnp.int32, (16, 1), 0)
        ids = jnp.where(ids < 0, ids + height, ids)
        ids = jnp.where(ids >= height, ids - height, ids)
        up = jnp.where(ids == 0, 0.0, piece[7:23])
        down = jnp.where(ids == height - 1, 0.0, piece[9:25])
        left = jnp.where(cols == 0, 0.0, pltpu.roll(mid, 1, 1))
        right = jnp.where(cols == width - 1, 0.0, pltpu.roll(mid, width - 1, 1))
        inside = (ids >= low_row) & (ids < high_row)
        cell = jnp.where(inside, mid - 0.25 * (up + down + left + right), 0.0)
        for parity in range(2):
            if parity == 0:
                fold = cell[:, :half] + cell[:, half:]
            else:
                fold = cell[:, :half] - cell[:, half:]
            hi, lo = split(fold)
            ch[parity, pl.ds(at, 16), :] = hi
            cl[parity, pl.ds(at, 16), :] = lo
        return carry

    lax.fori_loop(1, rows // 16, clean, 0)
    for n in range(2):
        halo_copy(n).wait()
    lax.fori_loop(0, 2, lambda n, carry: clean(n * (rows // 16), carry), 0)

    def step(s, carry):
        for copy in table_copies(s):
            copy.wait()
        t = tile_at(s)
        for parity in range(2):
            grid[parity] = (
                dot(ch[parity], bufh[s, parity])
                + dot(ch[parity], bufl[s, parity])
                + dot(cl[parity], bufh[s, parity])
            )

        def fir(i, inner):
            at = pl.multiple_of(i * 32, 32)
            for parity in range(2):
                re = grid[parity, pl.ds(at, 48), :TILE]
                im = grid[parity, pl.ds(at, 48), TILE:]
                sums = [jnp.zeros((32, TILE), F32) for _ in range(3)]
                for k in range(8):
                    shift_re = re[k : k + 40]
                    shift_im = im[k : k + 40]
                    shifted = (shift_re + shift_im, shift_im, shift_re)
                    for a in (k, k + 8):
                        for n in range(3):
                            tap = taps[t, parity, n, a : a + 1, :]
                            sums[n] = sums[n] + tap * shifted[n][a - k : a - k + 32]
                lane = parity * 2 * TILE
                work[s, pl.ds(at, 32), lane : lane + TILE] = sums[0] + sums[1]
                work[s, pl.ds(at, 32), lane + TILE : lane + 2 * TILE] = sums[0] - sums[2]
            return inner

        @pl.when(s == 1)
        def _():
            pair_copy(0).wait_recv()

        for c in range(CHUNKS):
            lax.fori_loop(c * (chunk // 32), (c + 1) * (chunk // 32), fir, 0)

            @pl.when(s == 1)
            def _(c=c):
                part = pl.ds(c * chunk, chunk)
                work[1, part, :] = work[1, part, :] + pair_in[0, part, :]
                read_copy(c).start()

            @pl.when(s == 3)
            def _(c=c):
                if c == 0:
                    pair_copy(1).wait_recv()
                if c > 0:
                    send(c - 1)

        @pl.when(s % 2 == 0)
        def _():
            pair_copy(s // 2).start()

        return carry

    lanes = lax.broadcasted_iota(jnp.int32, (32, TILE), 1) // share

    def send(c):
        read_copy(c).wait_recv()

        def pack(i, carry):
            part = pl.ds(pl.multiple_of(c * chunk + i * 32, 32), 32)
            total = work[3, part, :] + pair_in[1, part, :] + read_in[part, :]
            quads = [total[:, q * TILE : (q + 1) * TILE] for q in (0, 2, 1, 3)]
            for to in range(freqs):
                result = None
                for q in range(4):
                    shift = (q - to) * share % TILE
                    moved = quads[q] if shift == 0 else pltpu.roll(quads[q], shift, 1)
                    result = moved if q == 0 else jnp.where(lanes == q, moved, result)
                freq_out[to, part, :] = result
            return carry

        lax.fori_loop(0, chunk // 32, pack, 0)
        for d in range(1, freqs):
            freq_copy(d, c).start()

    lax.fori_loop(0, 4, step, 0)
    send(CHUNKS - 1)
    freq_in[f] = freq_out[f]

    wide = 2 * TILE
    q = jnp.dot(
        stamps[...].reshape(count * stamp_len, stamp_len), psf_cols[f],
        precision=HIGHEST, preferred_element_type=F32,
    )
    rh, rl = split(psf_rows[reader])
    total = jnp.zeros((rows, wide), F32)
    for e in range(count):
        q_re = q[e * stamp_len : (e + 1) * stamp_len, :wide]
        q_im = q[e * stamp_len : (e + 1) * stamp_len, wide:]
        both = jnp.concatenate(
            [jnp.concatenate([q_re, q_im], axis=1), jnp.concatenate([q_im, -q_re], axis=1)], axis=0
        )
        qh, ql = split(both)
        psf = dot(rh, qh) + dot(rh, ql) + dot(rl, qh)
        gain = gate(e) * spread(zero_point[e]) / spread(noise_var[e])
        total = total + gain * (psf[:, :wide] * psf[:, :wide] + psf[:, wide:] * psf[:, wide:])
    total = lax.rsqrt(total)
    for side in range(2):
        inverse[side] = total[:, side * TILE : (side + 1) * TILE]

    for copy in col_copies:
        copy.wait()
    for c in range(CHUNKS):
        for d in range(1, freqs):
            freq_copy(d, c).wait_recv()
        parts = []
        for g in range(4):
            hi, lo = split(freq_in[g, pl.ds(c * chunk, chunk), :])
            parts.append(dot(hi, order[...]) + dot(lo, order[...]))
        for j in range(4):
            if j % 2 == 0:
                even, odd = parts[0] + parts[2], parts[1] + parts[3]
                mix = even + odd if j == 0 else even - odd
                top, low = mix[:, :TILE], mix[:, TILE:]
            else:
                even, odd = parts[0] - parts[2], parts[1] - parts[3]
                sign = 1.0 if j == 1 else -1.0
                top = even[:, :TILE] + sign * odd[:, TILE:]
                low = even[:, TILE:] - sign * odd[:, :TILE]
            hi, lo = split(jnp.concatenate([top, low], axis=0))
            at = c * 2 * chunk
            both = dot(colh[j, :, at : at + 2 * chunk], jnp.concatenate([hi, lo], axis=1))
            both = both[:, :TILE] + both[:, TILE:] + dot(coll[j, :, at : at + 2 * chunk], hi)
            col_out[j] = both if c == 0 else col_out[j] + both
            if c == CHUNKS - 1:
                for e in (1, 2, 0):
                    last_copy(e, j).start()

    lanes = lax.broadcasted_iota(jnp.int32, (TILE, TILE), 1)
    for j in range(4):
        last_in[reader, j] = col_out[j, pl.ds(pl.multiple_of(reader * TILE, TILE), TILE), :]
        for e in range(3):
            last_copy(e, j).wait_recv()
        for side in range(2):
            one, two = last_in[2 * side, j], last_in[2 * side + 1, j]
            re = jnp.where(lanes < TILE // 2, one, pltpu.roll(two, TILE // 2, 1))
            im = jnp.where(lanes < TILE // 2, pltpu.roll(one, TILE // 2, 1), two)
            place = pl.ds(j, TILE, stride=4)
            gain = inverse[side, place, :]
            stage[0, side, place, :] = re * gain
            stage[1, side, place, :] = im * gain

    for part in range(2):
        for side in range(2):
            out[part, :, side * TILE : (side + 1) * TILE] = stage[part, side]

    for n in range(2):
        pair_copy(n).wait_send()
    for c in range(CHUNKS):
        read_copy(c).wait_send()
        for d in range(1, freqs):
            freq_copy(d, c).wait_send()
    for e in range(3):
        for j in range(4):
            last_copy(e, j).wait_send()


def fused(scalars, stamps, ids, block, freqs, readers):
    rows, width = block.shape
    half = width // 2
    height = rows * freqs
    stamp_len = stamps.shape[1]
    offsets = np.arange(stamp_len) - stamp_len // 2
    phase = angles(offsets, ids.reshape(-1), width)
    tap_table = np.concatenate([np.cos(phase), -np.sin(phase)], axis=1).astype(np.float32)
    phase = angles(np.arange(height), offsets, height)
    psf_rows = np.concatenate([np.cos(phase), np.sin(phase)], axis=1).astype(np.float32)
    psf_rows = psf_rows.reshape(readers, height // readers, -1)
    phase = angles(offsets, np.arange(half), width).reshape(stamp_len, freqs, -1)
    psf_cols = np.concatenate([np.cos(phase), -np.sin(phase)], axis=2).astype(np.float32)
    psf_cols = psf_cols.transpose(1, 0, 2)
    order = order_matrix(TILE // 2)
    vmem = pl.BlockSpec(memory_space=pltpu.VMEM)
    smem = pl.BlockSpec(memory_space=pltpu.SMEM)
    anywhere = pl.BlockSpec(memory_space=pl.ANY)
    dma = pltpu.SemaphoreType.DMA
    return pl.pallas_call(
        functools.partial(fused_kernel, freqs),
        out_shape=jax.ShapeDtypeStruct((2, rows, 2 * TILE), F32),
        in_specs=[smem] * 5 + [vmem] * 5 + [anywhere] * 5,
        out_specs=vmem,
        scratch_shapes=[
            pltpu.VMEM((rows + 2 * HALO, width), F32),
            pltpu.VMEM((2, rows + 16, half), BF16),
            pltpu.VMEM((2, rows + 16, half), BF16),
            pltpu.VMEM((2, rows + 16, 2 * TILE), F32),
            pltpu.VMEM((4, 2, half, 2 * TILE), BF16),
            pltpu.VMEM((4, 2, half, 2 * TILE), BF16),
            pltpu.VMEM((4, rows, 4 * TILE), F32),
            pltpu.VMEM((2, rows, 4 * TILE), F32),
            pltpu.VMEM((rows, 4 * TILE), F32),
            pltpu.VMEM((freqs, rows, TILE), F32),
            pltpu.VMEM((freqs, rows, TILE), F32),
            pltpu.VMEM((4, 2, 3, stamp_len, TILE), F32),
            pltpu.VMEM((4, rows, 2 * rows), BF16),
            pltpu.VMEM((4, rows, 2 * rows), BF16),
            pltpu.VMEM((2, 2, rows, TILE), F32),
            pltpu.VMEM((4, rows, TILE), F32),
            pltpu.VMEM((4, 4, TILE, TILE), F32),
            pltpu.VMEM((2, rows, TILE), F32),
            dma,
            dma((2, 4)),
            dma((2,)),
            dma((2,)),
            dma((2,)),
            dma((2,)),
            dma((2,)),
            dma((CHUNKS,)),
            dma((CHUNKS,)),
            dma((freqs - 1, CHUNKS)),
            dma((freqs - 1, CHUNKS)),
            dma((3, 4)),
            dma((3, 4)),
        ],
        compiler_params=pltpu.CompilerParams(
            collective_id=0, has_side_effects=True, vmem_limit_bytes=58 * 1024 * 1024
        ),
        name="fused",
    )(
        *scalars, stamps, tap_table, psf_rows, psf_cols, order, block,
        *row_tables(ids, width), *column_tables(height, CHUNKS),
    )


def column_tables(height, chunks=1):
    quarter = height // 4
    inner = np.arange(quarter)
    parts = []
    for j in range(4):
        phase = angles(4 * np.arange(quarter) + j, inner, height)
        both = np.stack([np.cos(phase), np.sin(phase)], axis=1)
        both = both.reshape(quarter, 2, chunks, -1).transpose(0, 2, 1, 3)
        parts.append(both.reshape(quarter, -1))
    return split_np(np.stack(parts))


def order_matrix(share):
    size = 2 * share
    table = np.zeros((size, 2 * size), np.float32)
    for part in range(2):
        for parity in range(2):
            for j in range(share // 2):
                source = part * share + parity * (share // 2) + j
                place = 2 * j + parity
                table[source, part * share + place] = 1.0
                table[source, size + (1 - part) * share + place] = -1.0 if part == 0 else 1.0
    return table.astype(ml_dtypes.bfloat16)


def column_kernel(x, order, th, tl, out):
    height, lanes = x.shape
    quarter = height // 4
    step = pl.program_id(0)
    for j in range(4):

        @pl.when(step == j)
        def _(j=j):
            parts = []
            for f in range(4):
                hi, lo = split(x[f * quarter : (f + 1) * quarter])
                parts.append(dot(hi, order[...]) + dot(lo, order[...]))
            if j % 2 == 0:
                even, odd = parts[0] + parts[2], parts[1] + parts[3]
                mix = even + odd if j == 0 else even - odd
                top, low = mix[:, :lanes], mix[:, lanes:]
            else:
                even, odd = parts[0] - parts[2], parts[1] - parts[3]
                sign = 1.0 if j == 1 else -1.0
                top = even[:, :lanes] + sign * odd[:, lanes:]
                low = even[:, lanes:] - sign * odd[:, :lanes]
            both = jnp.concatenate([top, low], axis=0)
            hi, lo = split(both)
            wide = dot(th[0], jnp.concatenate([hi, lo], axis=1))
            result = wide[:, :lanes] + wide[:, lanes:] + dot(tl[0], hi)
            out[pl.ds(j, quarter, stride=4), :] = result


def columns(x, order, tables):
    height, lanes = x.shape
    quarter = height // 4
    table_spec = pl.BlockSpec((1, quarter, 2 * quarter), lambda j: (j, 0, 0))
    return pl.pallas_call(
        column_kernel,
        grid=(4,),
        out_shape=jax.ShapeDtypeStruct((height, lanes), F32),
        in_specs=[
            pl.BlockSpec((height, lanes), lambda j: (0, 0)),
            pl.BlockSpec((lanes, 2 * lanes), lambda j: (0, 0)),
            table_spec,
            table_spec,
        ],
        out_specs=pl.BlockSpec((height, lanes), lambda j: (0, 0)),
        compiler_params=pltpu.CompilerParams(vmem_limit_bytes=48 * 1024 * 1024),
        name="columns",
    )(x, order, *tables)


def denom_kernel(weight, rows, cols, out):
    count = cols.shape[0]
    lanes = out.shape[1]
    total = jnp.zeros(out.shape, F32)
    rh, rl = split(rows[...])
    for e in range(count):
        chh, cll = split(cols[e])
        psf = dot(rh, chh) + dot(rh, cll) + dot(rl, chh)
        total = total + weight[e] * (psf[:, :lanes] * psf[:, :lanes] + psf[:, lanes:] * psf[:, lanes:])
    out[...] = lax.rsqrt(total)


def per_device(exposures, stamps, zero_point, noise_var, footprint, accept, assign):
    exp_dev, rows_dev, width = exposures.shape
    freqs = lax.axis_size("freq")
    readers = lax.axis_size(READERS)
    height = rows_dev * freqs
    per_freq = width // 2 // freqs
    share = per_freq // readers
    out_rows = height // readers
    stamp_len = stamps.shape[1]
    count_all = assign.shape[0]
    freq_at = lax.axis_index("freq")
    reader_at = lax.axis_index(READERS)
    ids = column_order(width, freqs, readers)
    tiles = ids.shape[1]
    offsets = np.arange(stamp_len) - stamp_len // 2

    block = exposures[0]
    square = lax.axis_size("read") == 2 and lax.axis_size("pair") == 2
    if square and tiles == 4 and freqs == 4 and rows_dev == 4 * TILE:
        scalars = (assign, footprint, accept, zero_point, noise_var)
        return fused(scalars, stamps, ids, block, freqs, readers)
    forward = [(i, (i + 1) % freqs) for i in range(freqs)]
    backward = [(t, s) for s, t in forward]
    low = lax.ppermute(block[rows_dev - HALO :], "freq", forward)
    high = lax.ppermute(block[:HALO], "freq", backward)

    labels = jnp.arange(count_all, dtype=jnp.int32)
    owner = jnp.sum(jnp.where(labels == reader_at, assign, 0))
    chosen = labels == owner
    low_row = jnp.sum(jnp.where(chosen, footprint[:, 0], 0))
    high_row = jnp.sum(jnp.where(chosen, footprint[:, 1], 0))
    accepted = accept.astype(F32)
    numer_weight = accepted * zero_point / noise_var
    denom_weight = accepted * zero_point * zero_point / noise_var
    scale = 1.0 / math.sqrt(height * width)
    weight = jnp.sum(jnp.where(chosen, numer_weight, 0.0)) * scale
    stamp = jnp.sum(jnp.where(chosen[:, None, None], stamps, 0.0), axis=0) * weight
    tap_phase = angles(offsets, ids.reshape(-1), width)
    tap_table = np.stack([np.cos(tap_phase), -np.sin(tap_phase)]).astype(np.float32)
    taps = jnp.einsum("ab,cbp->cap", stamp, tap_table, precision=HIGHEST)
    taps = taps.reshape(2, stamp_len, 2, tiles, TILE).transpose(3, 2, 0, 1, 4)
    info = jnp.stack([freq_at * rows_dev, low_row, high_row, jnp.int32(height)]).astype(jnp.int32)

    tables = row_tables(ids, width)
    terms = front(info, low, block, high, taps, tables)
    if tiles != readers:
        terms = terms.reshape(tiles, rows_dev, 2, 2, readers // tiles, TILE * tiles // readers)
        terms = terms.transpose(0, 4, 1, 2, 3, 5).reshape(readers, rows_dev, -1)
    summed = lax.psum_scatter(terms, READERS, scatter_dimension=0, tiled=True)
    summed = summed.reshape(rows_dev, 2, 2, freqs, share // 2)
    summed = summed.transpose(3, 0, 2, 1, 4).reshape(freqs, rows_dev, 2 * share)
    gathered = lax.all_to_all(summed, "freq", split_axis=0, concat_axis=0, tiled=True)
    grid = columns(gathered.reshape(height, 2 * share), order_matrix(share), column_tables(height))
    grid = lax.all_to_all(
        grid.reshape(readers, out_rows, 2 * share), READERS, split_axis=0, concat_axis=0, tiled=True
    )
    numer = grid.reshape(readers, out_rows, 2, share).transpose(2, 1, 0, 3)
    numer = numer.reshape(2, out_rows, per_freq)

    all_u = angles(np.arange(height), offsets, height)
    all_rows = np.concatenate([np.cos(all_u), np.sin(all_u)], axis=1).astype(np.float32)
    psf_rows = lax.dynamic_slice_in_dim(jnp.asarray(all_rows), reader_at * out_rows, out_rows, 0)
    all_v = angles(offsets, np.arange(width // 2), width)
    all_cols = np.stack([np.cos(all_v), -np.sin(all_v)]).astype(np.float32)
    own_cols = lax.dynamic_slice_in_dim(jnp.asarray(all_cols), freq_at * per_freq, per_freq, 2)
    q = jnp.einsum("nab,cbp->cnap", stamps, own_cols, precision=HIGHEST)
    psf_cols = jnp.concatenate(
        [jnp.concatenate([q[0], q[1]], axis=2), jnp.concatenate([q[1], -q[0]], axis=2)], axis=1
    )
    inverse = pl.pallas_call(
        denom_kernel,
        out_shape=jax.ShapeDtypeStruct((out_rows, per_freq), F32),
        in_specs=[
            pl.BlockSpec(memory_space=pltpu.SMEM),
            pl.BlockSpec(memory_space=pltpu.VMEM),
            pl.BlockSpec(memory_space=pltpu.VMEM),
        ],
        out_specs=pl.BlockSpec(memory_space=pltpu.VMEM),
        compiler_params=pltpu.CompilerParams(vmem_limit_bytes=32 * 1024 * 1024),
        name="denom",
    )(denom_weight, psf_rows, psf_cols)
    return numer * inverse


def solution(mesh):
    in_specs = (
        P(("groups", "read", "pair"), "freq", None),
        P("groups", None, None),
        P("groups"),
        P("groups"),
        P("groups", None),
        P("groups"),
        P("groups"),
    )
    out_specs = P(None, ("groups", "read", "pair"), "freq")
    return jax.shard_map(
        per_device, mesh=mesh, in_specs=in_specs, out_specs=out_specs, check_vma=False
    )
```

```python
import functools
import math

import jax
import jax.numpy as jnp
import ml_dtypes
import numpy as np
from jax import lax
from jax.experimental import pallas as pl
from jax.experimental.pallas import tpu as pltpu
from jax.sharding import PartitionSpec as P

HIGHEST = lax.Precision.HIGHEST
TWO_PI = 2.0 * math.pi
HALO = 16
TILE = 128
BF16 = jnp.bfloat16
F32 = jnp.float32
READERS = ("read", "pair")


def split_np(table):
    hi = table.astype(np.float32).astype(ml_dtypes.bfloat16)
    lo = (table - hi.astype(np.float64)).astype(np.float32).astype(ml_dtypes.bfloat16)
    return hi, lo


def split(value):
    hi = value.astype(BF16)
    return hi, (value - hi.astype(F32)).astype(BF16)


def angles(left, right, modulus):
    return (np.outer(left, right) % modulus).astype(np.float64) * (TWO_PI / modulus)


def dot(left, right):
    return jnp.dot(left, right, preferred_element_type=F32)


def column_order(width, freqs, readers):
    share = width // 2 // freqs // readers
    parity = np.arange(2)[:, None, None, None]
    reader = np.arange(readers)[None, :, None, None]
    freq = np.arange(freqs)[None, None, :, None]
    inner = np.arange(share // 2)[None, None, None, :]
    ids = freq * (share * readers) + reader * share + 2 * inner + parity
    return ids.reshape(2, -1, TILE)


def row_tables(ids, width):
    half = np.arange(width // 2)
    parts = []
    for tile in range(ids.shape[1]):
        both = []
        for parity in range(2):
            phase = angles(half, ids[parity, tile], width)
            both.append(np.concatenate([np.cos(phase), -np.sin(phase)], axis=1))
        parts.append(np.stack(both))
    return split_np(np.stack(parts))


def front_kernel(info, low, block, high, taps, th, tl, out, ext, ch, cl, grid):
    rows, width = block.shape
    half = width // 2
    height = info[3]

    @pl.when(pl.program_id(0) == 0)
    def _():
        ext[:HALO] = low[...]
        ext[HALO : HALO + rows] = block[...]
        ext[HALO + rows :] = high[...]
        cols = lax.broadcasted_iota(jnp.int32, (16, width), 1)

        def clean(i, carry):
            at = pl.multiple_of(i * 16, 16)
            piece = ext[pl.ds(at, 32), :]
            mid = piece[8:24]
            ids = info[0] - 8 + at + lax.broadcasted_iota(jnp.int32, (16, 1), 0)
            ids = jnp.where(ids < 0, ids + height, ids)
            ids = jnp.where(ids >= height, ids - height, ids)
            up = jnp.where(ids == 0, 0.0, piece[7:23])
            down = jnp.where(ids == height - 1, 0.0, piece[9:25])
            left = jnp.where(cols == 0, 0.0, pltpu.roll(mid, 1, 1))
            right = jnp.where(cols == width - 1, 0.0, pltpu.roll(mid, width - 1, 1))
            inside = (ids >= info[1]) & (ids < info[2])
            cell = jnp.where(inside, mid - 0.25 * (up + down + left + right), 0.0)
            for parity in range(2):
                if parity == 0:
                    fold = cell[:, :half] + cell[:, half:]
                else:
                    fold = cell[:, :half] - cell[:, half:]
                hi, lo = split(fold)
                ch[parity, pl.ds(at, 16), :] = hi
                cl[parity, pl.ds(at, 16), :] = lo
            return carry

        lax.fori_loop(0, (rows + 16) // 16, clean, 0)

    for parity in range(2):
        grid[parity] = (
            dot(ch[parity], th[0, parity])
            + dot(ch[parity], tl[0, parity])
            + dot(cl[parity], th[0, parity])
        )

    def fir(i, carry):
        at = pl.multiple_of(i * 32, 32)
        for parity in range(2):
            re = grid[parity, pl.ds(at, 48), :TILE]
            im = grid[parity, pl.ds(at, 48), TILE:]
            sum_re = jnp.zeros((32, TILE), F32)
            sum_im = jnp.zeros((32, TILE), F32)
            for k in range(8):
                shift_re = re[k : k + 40]
                shift_im = im[k : k + 40]
                for a in (k, k + 8):
                    qr = taps[0, parity, 0, a : a + 1, :]
                    qi = taps[0, parity, 1, a : a + 1, :]
                    xr = shift_re[a - k : a - k + 32]
                    xi = shift_im[a - k : a - k + 32]
                    sum_re = sum_re + (qr * xr + qi * xi)
                    sum_im = sum_im + (qr * xi - qi * xr)
            lane = parity * 2 * TILE
            out[0, pl.ds(at, 32), lane : lane + TILE] = sum_re
            out[0, pl.ds(at, 32), lane + TILE : lane + 2 * TILE] = sum_im
        return carry

    lax.fori_loop(0, rows // 32, fir, 0)


def front(info, low, block, high, taps, tables):
    rows, width = block.shape
    tiles = tables[0].shape[0]
    whole = lambda shape: pl.BlockSpec(shape, lambda t: (0,) * len(shape))
    table_spec = pl.BlockSpec((1, 2, width // 2, 2 * TILE), lambda t: (t, 0, 0, 0))
    return pl.pallas_call(
        front_kernel,
        grid=(tiles,),
        out_shape=jax.ShapeDtypeStruct((tiles, rows, 4 * TILE), F32),
        in_specs=[
            pl.BlockSpec(memory_space=pltpu.SMEM),
            whole((HALO, width)),
            whole((rows, width)),
            whole((HALO, width)),
            pl.BlockSpec((1, 2, 2, taps.shape[3], TILE), lambda t: (t, 0, 0, 0, 0)),
            table_spec,
            table_spec,
        ],
        out_specs=pl.BlockSpec((1, rows, 4 * TILE), lambda t: (t, 0, 0)),
        scratch_shapes=[
            pltpu.VMEM((rows + 2 * HALO, width), F32),
            pltpu.VMEM((2, rows + 16, width // 2), BF16),
            pltpu.VMEM((2, rows + 16, width // 2), BF16),
            pltpu.VMEM((2, rows + 16, 2 * TILE), F32),
        ],
        compiler_params=pltpu.CompilerParams(vmem_limit_bytes=48 * 1024 * 1024),
        name="front",
    )(info, low, block, high, taps, *tables)


CHUNKS = 8
MESH = pl.DeviceIdType.MESH


def fused_kernel(
    freqs, assign, footprint, accept, zero_point, noise_var,
    stamps, tap_table, psf_rows, psf_cols, order, block, th, tl, uh, ul, out,
    ext, ch, cl, grid, bufh, bufl, work, pair_in, read_in, freq_out, freq_in,
    taps, colh, coll, stage, col_out, last_in, inverse,
    block_sem, table_sem, col_sem, halo_send, halo_recv, pair_send, pair_recv,
    read_send, read_recv, freq_send, freq_recv, last_send, last_recv,
):
    rows, width = block.shape
    half = width // 2
    height = rows * freqs
    chunk = rows // CHUNKS
    share = TILE // freqs
    count, stamp_len, _ = stamps.shape
    r = lax.axis_index("read")
    p = lax.axis_index("pair")
    f = lax.axis_index("freq")
    reader = r * 2 + p

    def tile_at(s):
        rd = jnp.where(s < 2, 1 - r, r)
        pd = jnp.where(s % 2 == 0, 1 - p, p)
        return rd * 2 + pd

    def table_copies(s):
        t = tile_at(s)
        return (
            pltpu.make_async_copy(th.at[t], bufh.at[s], table_sem.at[0, s]),
            pltpu.make_async_copy(tl.at[t], bufl.at[s], table_sem.at[1, s]),
        )

    col_copies = (
        pltpu.make_async_copy(uh, colh, col_sem.at[0]),
        pltpu.make_async_copy(ul, coll, col_sem.at[1]),
    )
    block_copy = pltpu.make_async_copy(block, ext.at[pl.ds(HALO, rows)], block_sem)

    def halo_copy(n):
        source = rows - HALO if n == 0 else 0
        place = 0 if n == 0 else HALO + rows
        to = lax.rem(f + (1 if n == 0 else freqs - 1), freqs)
        return pltpu.make_async_remote_copy(
            src_ref=block.at[pl.ds(source, HALO)], dst_ref=ext.at[pl.ds(place, HALO)],
            send_sem=halo_send.at[n], recv_sem=halo_recv.at[n],
            device_id={"freq": to}, device_id_type=MESH,
        )

    def pair_copy(n):
        return pltpu.make_async_remote_copy(
            src_ref=work.at[2 * n], dst_ref=pair_in.at[n],
            send_sem=pair_send.at[n], recv_sem=pair_recv.at[n],
            device_id={"pair": 1 - p}, device_id_type=MESH,
        )

    def read_copy(c):
        part = pl.ds(c * chunk, chunk)
        return pltpu.make_async_remote_copy(
            src_ref=work.at[1, part], dst_ref=read_in.at[part],
            send_sem=read_send.at[c], recv_sem=read_recv.at[c],
            device_id={"read": 1 - r}, device_id_type=MESH,
        )

    def freq_copy(d, c):
        part = pl.ds(c * chunk, chunk)
        to = lax.rem(f + d, freqs)
        return pltpu.make_async_remote_copy(
            src_ref=freq_out.at[to, part], dst_ref=freq_in.at[f, part],
            send_sem=freq_send.at[d - 1, c], recv_sem=freq_recv.at[d - 1, c],
            device_id={"freq": to}, device_id_type=MESH,
        )

    def last_copy(e, j):
        rd = r if e == 0 else 1 - r
        pd = p if e == 1 else 1 - p
        return pltpu.make_async_remote_copy(
            src_ref=col_out.at[j, pl.ds(pl.multiple_of((rd * 2 + pd) * TILE, TILE), TILE)],
            dst_ref=last_in.at[reader, j],
            send_sem=last_send.at[e, j], recv_sem=last_recv.at[e, j],
            device_id={"read": rd, "pair": pd}, device_id_type=MESH,
        )

    barrier = pltpu.get_barrier_semaphore()
    for to in (
        {"pair": 1 - p},
        {"read": 1 - r},
        {"read": 1 - r, "pair": 1 - p},
        *({"freq": lax.rem(f + d, freqs)} for d in range(1, freqs)),
    ):
        pl.semaphore_signal(barrier, inc=1, device_id=to, device_id_type=MESH)
    block_copy.start()
    for s in range(4):
        for copy in table_copies(s):
            copy.start()
    for copy in col_copies:
        copy.start()
    pl.semaphore_wait(barrier, freqs + 2)
    for n in range(2):
        halo_copy(n).start()

    owner = assign[reader]
    low_row = footprint[owner, 0]
    high_row = footprint[owner, 1]

    def spread(value):
        return jnp.full((1, 2 * TILE), value, F32)

    def gate(e):
        return spread(accept[e].astype(F32)) * spread(zero_point[e])

    weight = gate(owner) / spread(noise_var[owner]) * (1.0 / math.sqrt(height * width))
    all_taps = jnp.dot(stamps[owner], tap_table[...], precision=HIGHEST, preferred_element_type=F32)
    for parity in range(2):
        for t in range(4):
            at = (parity * 4 + t) * TILE
            re = all_taps[:, at : at + TILE] * weight[:, :TILE]
            im = all_taps[:, half + at : half + at + TILE] * weight[:, :TILE]
            taps[t, parity, 0] = re
            taps[t, parity, 1] = im - re
            taps[t, parity, 2] = im + re

    block_copy.wait()
    cols = lax.broadcasted_iota(jnp.int32, (16, width), 1)

    def clean(i, carry):
        at = pl.multiple_of(i * 16, 16)
        piece = ext[pl.ds(at, 32), :]
        mid = piece[8:24]
        ids = f * rows - 8 + at + lax.broadcasted_iota(jnp.int32, (16, 1), 0)
        ids = jnp.where(ids < 0, ids + height, ids)
        ids = jnp.where(ids >= height, ids - height, ids)
        up = jnp.where(ids == 0, 0.0, piece[7:23])
        down = jnp.where(ids == height - 1, 0.0, piece[9:25])
        left = jnp.where(cols == 0, 0.0, pltpu.roll(mid, 1, 1))
        right = jnp.where(cols == width - 1, 0.0, pltpu.roll(mid, width - 1, 1))
        inside = (ids >= low_row) & (ids < high_row)
        cell = jnp.where(inside, mid - 0.25 * (up + down + left + right), 0.0)
        for parity in range(2):
            if parity == 0:
                fold = cell[:, :half] + cell[:, half:]
            else:
                fold = cell[:, :half] - cell[:, half:]
            hi, lo = split(fold)
            ch[parity, pl.ds(at, 16), :] = hi
            cl[parity, pl.ds(at, 16), :] = lo
        return carry

    lax.fori_loop(1, rows // 16, clean, 0)
    for n in range(2):
        halo_copy(n).wait()
    lax.fori_loop(0, 2, lambda n, carry: clean(n * (rows // 16), carry), 0)

    def step(s, carry):
        for copy in table_copies(s):
            copy.wait()
        t = tile_at(s)
        for parity in range(2):
            grid[parity] = (
                dot(ch[parity], bufh[s, parity])
                + dot(ch[parity], bufl[s, parity])
                + dot(cl[parity], bufh[s, parity])
            )

        def fir(i, inner):
            at = pl.multiple_of(i * 32, 32)
            for parity in range(2):
                re = grid[parity, pl.ds(at, 48), :TILE]
                im = grid[parity, pl.ds(at, 48), TILE:]
                sums = [jnp.zeros((32, TILE), F32) for _ in range(3)]
                for k in range(8):
                    shift_re = re[k : k + 40]
                    shift_im = im[k : k + 40]
                    shifted = (shift_re + shift_im, shift_im, shift_re)
                    for a in (k, k + 8):
                        for n in range(3):
                            tap = taps[t, parity, n, a : a + 1, :]
                            sums[n] = sums[n] + tap * shifted[n][a - k : a - k + 32]
                lane = parity * 2 * TILE
                work[s, pl.ds(at, 32), lane : lane + TILE] = sums[0] + sums[1]
                work[s, pl.ds(at, 32), lane + TILE : lane + 2 * TILE] = sums[0] - sums[2]
            return inner

        @pl.when(s == 1)
        def _():
            pair_copy(0).wait_recv()

        for c in range(CHUNKS):
            lax.fori_loop(c * (chunk // 32), (c + 1) * (chunk // 32), fir, 0)

            @pl.when(s == 1)
            def _(c=c):
                part = pl.ds(c * chunk, chunk)
                work[1, part, :] = work[1, part, :] + pair_in[0, part, :]
                read_copy(c).start()

            @pl.when(s == 3)
            def _(c=c):
                if c == 0:
                    pair_copy(1).wait_recv()
                if c > 0:
                    send(c - 1)

        @pl.when(s % 2 == 0)
        def _():
            pair_copy(s // 2).start()

        return carry

    lanes = lax.broadcasted_iota(jnp.int32, (32, TILE), 1) // share

    def send(c):
        read_copy(c).wait_recv()

        def pack(i, carry):
            part = pl.ds(pl.multiple_of(c * chunk + i * 32, 32), 32)
            total = work[3, part, :] + pair_in[1, part, :] + read_in[part, :]
            quads = [total[:, q * TILE : (q + 1) * TILE] for q in (0, 2, 1, 3)]
            for to in range(freqs):
                result = None
                for q in range(4):
                    shift = (q - to) * share % TILE
                    moved = quads[q] if shift == 0 else pltpu.roll(quads[q], shift, 1)
                    result = moved if q == 0 else jnp.where(lanes == q, moved, result)
                freq_out[to, part, :] = result
            return carry

        lax.fori_loop(0, chunk // 32, pack, 0)
        for d in range(1, freqs):
            freq_copy(d, c).start()

    lax.fori_loop(0, 4, step, 0)
    send(CHUNKS - 1)
    freq_in[f] = freq_out[f]

    wide = 2 * TILE
    q = jnp.dot(
        stamps[...].reshape(count * stamp_len, stamp_len), psf_cols[f],
        precision=HIGHEST, preferred_element_type=F32,
    )
    rh, rl = split(psf_rows[reader])
    total = jnp.zeros((rows, wide), F32)
    for e in range(count):
        q_re = q[e * stamp_len : (e + 1) * stamp_len, :wide]
        q_im = q[e * stamp_len : (e + 1) * stamp_len, wide:]
        both = jnp.concatenate(
            [jnp.concatenate([q_re, q_im], axis=1), jnp.concatenate([q_im, -q_re], axis=1)], axis=0
        )
        qh, ql = split(both)
        psf = dot(rh, qh) + dot(rh, ql) + dot(rl, qh)
        gain = gate(e) * spread(zero_point[e]) / spread(noise_var[e])
        total = total + gain * (psf[:, :wide] * psf[:, :wide] + psf[:, wide:] * psf[:, wide:])
    total = lax.rsqrt(total)
    for side in range(2):
        inverse[side] = total[:, side * TILE : (side + 1) * TILE]

    for copy in col_copies:
        copy.wait()
    for c in range(CHUNKS):
        for d in range(1, freqs):
            freq_copy(d, c).wait_recv()
        parts = []
        for g in range(4):
            hi, lo = split(freq_in[g, pl.ds(c * chunk, chunk), :])
            parts.append(dot(hi, order[...]) + dot(lo, order[...]))
        for j in range(4):
            if j % 2 == 0:
                even, odd = parts[0] + parts[2], parts[1] + parts[3]
                mix = even + odd if j == 0 else even - odd
                top, low = mix[:, :TILE], mix[:, TILE:]
            else:
                even, odd = parts[0] - parts[2], parts[1] - parts[3]
                sign = 1.0 if j == 1 else -1.0
                top = even[:, :TILE] + sign * odd[:, TILE:]
                low = even[:, TILE:] - sign * odd[:, :TILE]
            hi, lo = split(jnp.concatenate([top, low], axis=0))
            at = c * 2 * chunk
            both = dot(colh[j, :, at : at + 2 * chunk], jnp.concatenate([hi, lo], axis=1))
            both = both[:, :TILE] + both[:, TILE:] + dot(coll[j, :, at : at + 2 * chunk], hi)
            col_out[j] = both if c == 0 else col_out[j] + both
            if c == CHUNKS - 1:
                for e in (1, 2, 0):
                    last_copy(e, j).start()

    lanes = lax.broadcasted_iota(jnp.int32, (TILE, TILE), 1)
    for j in range(4):
        last_in[reader, j] = col_out[j, pl.ds(pl.multiple_of(reader * TILE, TILE), TILE), :]
        for e in range(3):
            last_copy(e, j).wait_recv()
        for side in range(2):
            one, two = last_in[2 * side, j], last_in[2 * side + 1, j]
            re = jnp.where(lanes < TILE // 2, one, pltpu.roll(two, TILE // 2, 1))
            im = jnp.where(lanes < TILE // 2, pltpu.roll(one, TILE // 2, 1), two)
            place = pl.ds(j, TILE, stride=4)
            gain = inverse[side, place, :]
            stage[0, side, place, :] = re * gain
            stage[1, side, place, :] = im * gain

    for part in range(2):
        for side in range(2):
            out[part, :, side * TILE : (side + 1) * TILE] = stage[part, side]

    for n in range(2):
        pair_copy(n).wait_send()
    for c in range(CHUNKS):
        read_copy(c).wait_send()
        for d in range(1, freqs):
            freq_copy(d, c).wait_send()
    for e in range(3):
        for j in range(4):
            last_copy(e, j).wait_send()


def fused(scalars, stamps, ids, block, freqs, readers):
    rows, width = block.shape
    half = width // 2
    height = rows * freqs
    stamp_len = stamps.shape[1]
    offsets = np.arange(stamp_len) - stamp_len // 2
    phase = angles(offsets, ids.reshape(-1), width)
    tap_table = np.concatenate([np.cos(phase), -np.sin(phase)], axis=1).astype(np.float32)
    phase = angles(np.arange(height), offsets, height)
    psf_rows = np.concatenate([np.cos(phase), np.sin(phase)], axis=1).astype(np.float32)
    psf_rows = psf_rows.reshape(readers, height // readers, -1)
    phase = angles(offsets, np.arange(half), width).reshape(stamp_len, freqs, -1)
    psf_cols = np.concatenate([np.cos(phase), -np.sin(phase)], axis=2).astype(np.float32)
    psf_cols = psf_cols.transpose(1, 0, 2)
    order = order_matrix(TILE // 2)
    vmem = pl.BlockSpec(memory_space=pltpu.VMEM)
    smem = pl.BlockSpec(memory_space=pltpu.SMEM)
    anywhere = pl.BlockSpec(memory_space=pl.ANY)
    dma = pltpu.SemaphoreType.DMA
    return pl.pallas_call(
        functools.partial(fused_kernel, freqs),
        out_shape=jax.ShapeDtypeStruct((2, rows, 2 * TILE), F32),
        in_specs=[smem] * 5 + [vmem] * 5 + [anywhere] * 5,
        out_specs=vmem,
        scratch_shapes=[
            pltpu.VMEM((rows + 2 * HALO, width), F32),
            pltpu.VMEM((2, rows + 16, half), BF16),
            pltpu.VMEM((2, rows + 16, half), BF16),
            pltpu.VMEM((2, rows + 16, 2 * TILE), F32),
            pltpu.VMEM((4, 2, half, 2 * TILE), BF16),
            pltpu.VMEM((4, 2, half, 2 * TILE), BF16),
            pltpu.VMEM((4, rows, 4 * TILE), F32),
            pltpu.VMEM((2, rows, 4 * TILE), F32),
            pltpu.VMEM((rows, 4 * TILE), F32),
            pltpu.VMEM((freqs, rows, TILE), F32),
            pltpu.VMEM((freqs, rows, TILE), F32),
            pltpu.VMEM((4, 2, 3, stamp_len, TILE), F32),
            pltpu.VMEM((4, rows, 2 * rows), BF16),
            pltpu.VMEM((4, rows, 2 * rows), BF16),
            pltpu.VMEM((2, 2, rows, TILE), F32),
            pltpu.VMEM((4, rows, TILE), F32),
            pltpu.VMEM((4, 4, TILE, TILE), F32),
            pltpu.VMEM((2, rows, TILE), F32),
            dma,
            dma((2, 4)),
            dma((2,)),
            dma((2,)),
            dma((2,)),
            dma((2,)),
            dma((2,)),
            dma((CHUNKS,)),
            dma((CHUNKS,)),
            dma((freqs - 1, CHUNKS)),
            dma((freqs - 1, CHUNKS)),
            dma((3, 4)),
            dma((3, 4)),
        ],
        compiler_params=pltpu.CompilerParams(
            collective_id=0, has_side_effects=True, vmem_limit_bytes=58 * 1024 * 1024
        ),
        name="fused",
    )(
        *scalars, stamps, tap_table, psf_rows, psf_cols, order, block,
        *row_tables(ids, width), *column_tables(height, CHUNKS),
    )


def column_tables(height, chunks=1):
    quarter = height // 4
    inner = np.arange(quarter)
    parts = []
    for j in range(4):
        phase = angles(4 * np.arange(quarter) + j, inner, height)
        both = np.stack([np.cos(phase), np.sin(phase)], axis=1)
        both = both.reshape(quarter, 2, chunks, -1).transpose(0, 2, 1, 3)
        parts.append(both.reshape(quarter, -1))
    return split_np(np.stack(parts))


def order_matrix(share):
    size = 2 * share
    table = np.zeros((size, 2 * size), np.float32)
    for part in range(2):
        for parity in range(2):
            for j in range(share // 2):
                source = part * share + parity * (share // 2) + j
                place = 2 * j + parity
                table[source, part * share + place] = 1.0
                table[source, size + (1 - part) * share + place] = -1.0 if part == 0 else 1.0
    return table.astype(ml_dtypes.bfloat16)


def column_kernel(x, order, th, tl, out):
    height, lanes = x.shape
    quarter = height // 4
    step = pl.program_id(0)
    for j in range(4):

        @pl.when(step == j)
        def _(j=j):
            parts = []
            for f in range(4):
                hi, lo = split(x[f * quarter : (f + 1) * quarter])
                parts.append(dot(hi, order[...]) + dot(lo, order[...]))
            if j % 2 == 0:
                even, odd = parts[0] + parts[2], parts[1] + parts[3]
                mix = even + odd if j == 0 else even - odd
                top, low = mix[:, :lanes], mix[:, lanes:]
            else:
                even, odd = parts[0] - parts[2], parts[1] - parts[3]
                sign = 1.0 if j == 1 else -1.0
                top = even[:, :lanes] + sign * odd[:, lanes:]
                low = even[:, lanes:] - sign * odd[:, :lanes]
            both = jnp.concatenate([top, low], axis=0)
            hi, lo = split(both)
            wide = dot(th[0], jnp.concatenate([hi, lo], axis=1))
            result = wide[:, :lanes] + wide[:, lanes:] + dot(tl[0], hi)
            out[pl.ds(j, quarter, stride=4), :] = result


def columns(x, order, tables):
    height, lanes = x.shape
    quarter = height // 4
    table_spec = pl.BlockSpec((1, quarter, 2 * quarter), lambda j: (j, 0, 0))
    return pl.pallas_call(
        column_kernel,
        grid=(4,),
        out_shape=jax.ShapeDtypeStruct((height, lanes), F32),
        in_specs=[
            pl.BlockSpec((height, lanes), lambda j: (0, 0)),
            pl.BlockSpec((lanes, 2 * lanes), lambda j: (0, 0)),
            table_spec,
            table_spec,
        ],
        out_specs=pl.BlockSpec((height, lanes), lambda j: (0, 0)),
        compiler_params=pltpu.CompilerParams(vmem_limit_bytes=48 * 1024 * 1024),
        name="columns",
    )(x, order, *tables)


def denom_kernel(weight, rows, cols, out):
    count = cols.shape[0]
    lanes = out.shape[1]
    total = jnp.zeros(out.shape, F32)
    rh, rl = split(rows[...])
    for e in range(count):
        chh, cll = split(cols[e])
        psf = dot(rh, chh) + dot(rh, cll) + dot(rl, chh)
        total = total + weight[e] * (psf[:, :lanes] * psf[:, :lanes] + psf[:, lanes:] * psf[:, lanes:])
    out[...] = lax.rsqrt(total)


def per_device(exposures, stamps, zero_point, noise_var, footprint, accept, assign):
    exp_dev, rows_dev, width = exposures.shape
    freqs = lax.axis_size("freq")
    readers = lax.axis_size(READERS)
    height = rows_dev * freqs
    per_freq = width // 2 // freqs
    share = per_freq // readers
    out_rows = height // readers
    stamp_len = stamps.shape[1]
    count_all = assign.shape[0]
    freq_at = lax.axis_index("freq")
    reader_at = lax.axis_index(READERS)
    ids = column_order(width, freqs, readers)
    tiles = ids.shape[1]
    offsets = np.arange(stamp_len) - stamp_len // 2

    block = exposures[0]
    square = lax.axis_size("read") == 2 and lax.axis_size("pair") == 2
    if square and tiles == 4 and freqs == 4 and rows_dev == 4 * TILE:
        scalars = (assign, footprint, accept, zero_point, noise_var)
        return fused(scalars, stamps, ids, block, freqs, readers)
    forward = [(i, (i + 1) % freqs) for i in range(freqs)]
    backward = [(t, s) for s, t in forward]
    low = lax.ppermute(block[rows_dev - HALO :], "freq", forward)
    high = lax.ppermute(block[:HALO], "freq", backward)

    labels = jnp.arange(count_all, dtype=jnp.int32)
    owner = jnp.sum(jnp.where(labels == reader_at, assign, 0))
    chosen = labels == owner
    low_row = jnp.sum(jnp.where(chosen, footprint[:, 0], 0))
    high_row = jnp.sum(jnp.where(chosen, footprint[:, 1], 0))
    accepted = accept.astype(F32)
    numer_weight = accepted * zero_point / noise_var
    denom_weight = accepted * zero_point * zero_point / noise_var
    scale = 1.0 / math.sqrt(height * width)
    weight = jnp.sum(jnp.where(chosen, numer_weight, 0.0)) * scale
    stamp = jnp.sum(jnp.where(chosen[:, None, None], stamps, 0.0), axis=0) * weight
    tap_phase = angles(offsets, ids.reshape(-1), width)
    tap_table = np.stack([np.cos(tap_phase), -np.sin(tap_phase)]).astype(np.float32)
    taps = jnp.einsum("ab,cbp->cap", stamp, tap_table, precision=HIGHEST)
    taps = taps.reshape(2, stamp_len, 2, tiles, TILE).transpose(3, 2, 0, 1, 4)
    info = jnp.stack([freq_at * rows_dev, low_row, high_row, jnp.int32(height)]).astype(jnp.int32)

    tables = row_tables(ids, width)
    terms = front(info, low, block, high, taps, tables)
    if tiles != readers:
        terms = terms.reshape(tiles, rows_dev, 2, 2, readers // tiles, TILE * tiles // readers)
        terms = terms.transpose(0, 4, 1, 2, 3, 5).reshape(readers, rows_dev, -1)
    summed = lax.psum_scatter(terms, READERS, scatter_dimension=0, tiled=True)
    summed = summed.reshape(rows_dev, 2, 2, freqs, share // 2)
    summed = summed.transpose(3, 0, 2, 1, 4).reshape(freqs, rows_dev, 2 * share)
    gathered = lax.all_to_all(summed, "freq", split_axis=0, concat_axis=0, tiled=True)
    grid = columns(gathered.reshape(height, 2 * share), order_matrix(share), column_tables(height))
    grid = lax.all_to_all(
        grid.reshape(readers, out_rows, 2 * share), READERS, split_axis=0, concat_axis=0, tiled=True
    )
    numer = grid.reshape(readers, out_rows, 2, share).transpose(2, 1, 0, 3)
    numer = numer.reshape(2, out_rows, per_freq)

    all_u = angles(np.arange(height), offsets, height)
    all_rows = np.concatenate([np.cos(all_u), np.sin(all_u)], axis=1).astype(np.float32)
    psf_rows = lax.dynamic_slice_in_dim(jnp.asarray(all_rows), reader_at * out_rows, out_rows, 0)
    all_v = angles(offsets, np.arange(width // 2), width)
    all_cols = np.stack([np.cos(all_v), -np.sin(all_v)]).astype(np.float32)
    own_cols = lax.dynamic_slice_in_dim(jnp.asarray(all_cols), freq_at * per_freq, per_freq, 2)
    q = jnp.einsum("nab,cbp->cnap", stamps, own_cols, precision=HIGHEST)
    psf_cols = jnp.concatenate(
        [jnp.concatenate([q[0], q[1]], axis=2), jnp.concatenate([q[1], -q[0]], axis=2)], axis=1
    )
    inverse = pl.pallas_call(
        denom_kernel,
        out_shape=jax.ShapeDtypeStruct((out_rows, per_freq), F32),
        in_specs=[
            pl.BlockSpec(memory_space=pltpu.SMEM),
            pl.BlockSpec(memory_space=pltpu.VMEM),
            pl.BlockSpec(memory_space=pltpu.VMEM),
        ],
        out_specs=pl.BlockSpec(memory_space=pltpu.VMEM),
        compiler_params=pltpu.CompilerParams(vmem_limit_bytes=32 * 1024 * 1024),
        name="denom",
    )(denom_weight, psf_rows, psf_cols)
    return numer * inverse


def solution(mesh):
    in_specs = (
        P(("groups", "read", "pair"), "freq", None),
        P("groups", None, None),
        P("groups"),
        P("groups"),
        P("groups", None),
        P("groups"),
        P("groups"),
    )
    out_specs = P(None, ("groups", "read", "pair"), "freq")
    return jax.shard_map(
        per_device, mesh=mesh, in_specs=in_specs, out_specs=out_specs, check_vma=False
    )
```
